256 devices in a mesh: dp: 4 (over z_hi), pipe: 8 (over x, core), tensor: 8 (over y, z_lo).
Axes of the slice: x: 4, y: 4, z: 8 (z_hi: 4, z_lo: 2; z = z_hi * 2 + z_lo), core: 2. Of those that a mesh axis runs over, the one named last changes fastest.
Arguments:
- activations: bfloat16 [4096, 28672], P('dp', 'tensor'), may hold values from -6 to 6
- down_weight: bfloat16 [28672, 8192], P('tensor', 'pipe'), may hold values from -0.03125 to 0.03125
- output_grads: bfloat16 [4096, 8192], P('dp', ('pipe', 'tensor')), may hold values from -170 to 170
- act_factors: bfloat16 [64, 32, 28672], P('pipe', None, 'tensor'), may hold values from -0.03125 to 0.03125
- grad_factors: bfloat16 [64, 32, 8192], P(None, None, ('pipe', 'tensor')), may hold values from -0.0625 to 0.0625
- rank_weight: float32 [64, 32], P('pipe'), may hold values from 0.05 to 1
Outputs:
- layer_output: bfloat16 [4096, 8192], P('dp', ('pipe', 'tensor'))
- influence: float32 [4096, 64], P('dp', 'pipe')
The draws below stay inside these ranges and needn't reach their ends.
All inputs are finite; a program needn't handle non-finite values.
Results may differ from the reference program's by a relative error of at most 0.001.
Values sent between devices are 32-bit elements; how exact they have to be, the bound alone decides.
No kernel may reach another device: no remote copies, remote signals or barrier semaphores. Data moves between devices by JAX's collectives and lax.ppermute only.
A program may use at most 128 MiB of HBM per device.

```python
import math
import jax
import jax.numpy as jnp
from jax import lax

D = 8192
FF = 28672
Q = 64
R = 32
TOKENS = 4096


def draw_output_grads(key, part):
    key = jax.random.fold_in(key, 5)
    position = jnp.arange(TOKENS, dtype=jnp.float32) / (TOKENS - 1)
    base = jnp.clip(jax.random.normal(key, (TOKENS, D), jnp.float32), -6.0, 6.0)
    scale = 10.0 ** position
    return (base * scale[:, None]).astype(jnp.bfloat16)


def block_levels(stream_key, dims, pieces, low, high):
    def one(dim, parts):
        draws = jax.random.uniform(jax.random.fold_in(jax.random.fold_in(stream_key, 6), dim), (parts,), jnp.float32, low / len(pieces), high / len(pieces))
        return jnp.repeat(jnp.exp(draws), dims[dim] // parts).reshape((-1,) + (1,) * (len(dims) - dim - 1))

    gain = one(*pieces[0])
    for cut in pieces[1:]:
        gain = gain * one(*cut)
    return gain


def scatter_about(own_key, dims, scale, most, shards=(), kind=jnp.bfloat16):
    result = jax.random.normal(own_key, dims, jnp.float32) * scale
    if len(shards) > 0:
        result = block_levels(own_key, dims, shards, -0.22, 0.18) * result
    return jnp.clip(result, min=-most, max=most).astype(kind)


def setup_inputs(seed: int = 0) -> dict:
    key_list = jax.random.split(jax.random.key(seed), 7)
    return {
        "activations": scatter_about(key_list[0], (TOKENS, FF), 1.0, 6.0, ((0, 4), (1, 8))),
        "down_weight": scatter_about(key_list[1], (FF, D), FF ** -0.5, 0.03125, ((0, 8), (1, 8))),
        "output_grads": draw_output_grads(jax.random.fold_in(key_list[6], 71), 0),
        "act_factors": scatter_about(key_list[3], (Q, R, FF), FF ** -0.5, 0.03125, ((0, 8), (2, 8))),
        "grad_factors": scatter_about(key_list[4], (Q, R, D), D ** -0.5, 0.0625, ((2, 64),)),
        "rank_weight": jnp.clip(jnp.exp(math.log(1.0) - 2.9957323 * jax.random.uniform(key_list[5], (Q, R), jnp.float32) ** block_levels(key_list[5], (Q, R), ((0, 8),), -0.2, 0.2)), 0.05, 1.0),
    }


def reference(activations, down_weight, output_grads, act_factors, grad_factors, rank_weight):
    layer_output = jnp.dot(activations, down_weight, preferred_element_type=jnp.float32).astype(jnp.bfloat16)
    act_proj = jnp.dot(activations, act_factors.reshape(Q * R, FF).T, preferred_element_type=jnp.float32)
    grad_proj = jnp.dot(output_grads, grad_factors.reshape(Q * R, D).T, preferred_element_type=jnp.float32)
    product = (act_proj * grad_proj).reshape(TOKENS, Q, R)
    raw_scores = lax.optimization_barrier(jnp.sum(product * rank_weight[None, :, :], axis=2)) * (1.0 / math.sqrt(R))
    spread = lax.optimization_barrier(jnp.mean(raw_scores * raw_scores, axis=0))
    influence = raw_scores / jnp.sqrt(spread + 1e-06)
    return (layer_output, influence)
```

```python
import functools
import math

import jax
import jax.numpy as jnp
from jax import lax
from jax.experimental import pallas as pl
from jax.experimental.pallas import tpu as pltpu
from jax.sharding import PartitionSpec as P

F32 = jnp.float32
MIB = 1 << 20


def x_shift(d):
    return [(p, ((p // 2 + d) % 4) * 2 + p % 2) for p in range(8)]


def core_swap():
    return [(p, p ^ 1) for p in range(8)]


def y_shift(d):
    return [(t, ((t // 2 + d) % 4) * 2 + t % 2) for t in range(8)]


def z_swap():
    return [(t, t ^ 1) for t in range(8)]


def dp_shift(d):
    return [(i, (i + d) % 4) for i in range(4)]


def params(limit):
    return pltpu.CompilerParams(vmem_limit_bytes=limit)


def cost(flops, nbytes):
    return pl.CostEstimate(flops=flops, bytes_accessed=nbytes, transcendentals=0)


def pack_kernel(idx, og, gf, *outs):
    tokens = og.shape[0]
    rows = gf.shape[0] // 4
    for out, d in zip(outs, (1, 3, 2)):
        out[pl.ds(0, tokens), :] = og[...].astype(F32)
        start = pl.multiple_of(lax.rem(idx[0] + d, 4) * rows, rows)
        out[pl.ds(tokens, rows), :] = gf[pl.ds(start, rows), :].astype(F32)


def pack(idx, og, gf):
    tokens, width = og.shape
    rows = tokens + gf.shape[0] // 4
    whole = pl.BlockSpec(memory_space=pltpu.VMEM)
    return pl.pallas_call(
        pack_kernel,
        grid_spec=pltpu.PrefetchScalarGridSpec(
            num_scalar_prefetch=1, grid=(), in_specs=[whole, whole], out_specs=[whole] * 3
        ),
        out_shape=[jax.ShapeDtypeStruct((rows, width), F32)] * 3,
        compiler_params=params(16 * MIB),
        cost_estimate=cost(0, 4 * 3 * rows * width),
        name="pack",
    )(idx, og, gf)


def act_kernel(idx, af, a, *rest):
    *outs, scratch = rest
    scratch[...] = lax.dot_general(
        af[...], a[...], (((1,), (1,)), ((), ())), preferred_element_type=F32
    )
    rows = outs[0].shape[0]
    for j, out in enumerate(outs):
        start = pl.multiple_of(lax.rem(idx[2] + j, 4) * rows, rows)
        out[...] = scratch[pl.ds(start, rows), :]


def act_pieces(idx, af, a):
    qr, hidden = af.shape
    tokens = a.shape[0]
    tile = 256
    return pl.pallas_call(
        act_kernel,
        grid_spec=pltpu.PrefetchScalarGridSpec(
            num_scalar_prefetch=1,
            grid=(tokens // tile,),
            in_specs=[
                pl.BlockSpec((qr, hidden), lambda i, idx: (0, 0)),
                pl.BlockSpec((tile, hidden), lambda i, idx: (i, 0)),
            ],
            out_specs=[pl.BlockSpec((qr // 4, tile), lambda i, idx: (0, i))] * 4,
            scratch_shapes=[pltpu.VMEM((qr, tile), F32)],
        ),
        out_shape=[jax.ShapeDtypeStruct((qr // 4, tokens), F32)] * 4,
        compiler_params=params(24 * MIB),
        cost_estimate=cost(2 * qr * tokens * hidden, 2 * hidden * (qr + tokens)),
        name="act",
    )(idx, af, a)


def layer_z_kernel(idx, a, w, keep, send):
    acc = jnp.dot(a[...], w[...], preferred_element_type=F32)
    half = acc.shape[1] // 2

    @pl.when(idx[3] == 0)
    def _():
        keep[0] = acc[:, :half]
        send[0] = acc[:, half:]

    @pl.when(idx[3] == 1)
    def _():
        keep[0] = acc[:, half:]
        send[0] = acc[:, :half]


def layer_z_first(idx, a, w, block, rows):
    hidden, cols = w.shape
    width = cols // 4
    return pl.pallas_call(
        layer_z_kernel,
        grid_spec=pltpu.PrefetchScalarGridSpec(
            num_scalar_prefetch=1,
            grid=(4,),
            in_specs=[
                pl.BlockSpec((rows, hidden), lambda j, idx: (block, 0)),
                pl.BlockSpec((hidden, width), lambda j, idx: (0, lax.rem(idx[2] + j, 4))),
            ],
            out_specs=[pl.BlockSpec((1, rows, width // 2), lambda j, idx: (j, 0, 0))] * 2,
        ),
        out_shape=[jax.ShapeDtypeStruct((4, rows, width // 2), F32)] * 2,
        compiler_params=params(24 * MIB),
        cost_estimate=cost(2 * rows * hidden * cols, 2 * hidden * (rows + cols)),
        name="layer_z",
    )(idx, a, w)


def layer_y_kernel(idx, a, w, *outs):
    for j, out in enumerate(outs):

        @pl.when(pl.program_id(0) == j)
        def _(out=out):
            out[...] = jnp.dot(a[...], w[...], preferred_element_type=F32)


def layer_y_first(idx, a, w, block, rows):
    hidden, cols = w.shape
    width = cols // 4
    return pl.pallas_call(
        layer_y_kernel,
        grid_spec=pltpu.PrefetchScalarGridSpec(
            num_scalar_prefetch=1,
            grid=(4,),
            in_specs=[
                pl.BlockSpec((rows, hidden), lambda j, idx: (block, 0)),
                pl.BlockSpec((hidden, width), lambda j, idx: (0, lax.rem(idx[2] + j, 4))),
            ],
            out_specs=[pl.BlockSpec((rows, width), lambda j, idx: (0, 0))] * 4,
        ),
        out_shape=[jax.ShapeDtypeStruct((rows, width), F32)] * 4,
        compiler_params=params(24 * MIB),
        cost_estimate=cost(2 * rows * hidden * cols, 2 * hidden * (rows + cols)),
        name="layer_y",
    )(idx, a, w)


def score_kernel(idx, og, gf, a1, b1, a2, b2, a3, b3, mine, other, out, *, ranks):
    bf = jnp.bfloat16
    lhs = jnp.concatenate([gf[...]] + [b[...].astype(bf) for b in (b1, b2, b3)], axis=1)
    rhs = jnp.concatenate([og[...]] + [a[...].astype(bf) for a in (a1, a2, a3)], axis=1)
    grad = lax.dot_general(lhs, rhs, (((1,), (1,)), ((), ())), preferred_element_type=F32)
    rows = mine.shape[1]
    parts = []
    for c in range(2):
        for b in range(4):
            j = lax.rem(b + 4 - idx[2], 4)
            act = jnp.where(idx[1] == c, mine[j], other[j])
            at = (c * 4 + b) * rows
            product = grad[at : at + rows, :] * act
            for q in range(rows // ranks):
                parts.append(
                    jnp.sum(product[q * ranks : (q + 1) * ranks], axis=0, keepdims=True)
                )
    out[...] = jnp.concatenate(parts, axis=0)


def scores(idx, og, gf, moved, mine, other, ranks):
    tokens, width = og.shape
    qr = gf.shape[0] // 4
    tile = 256
    first = tokens // qr
    in_specs = [
        pl.BlockSpec((tile, width), lambda i, idx: (i, 0)),
        pl.BlockSpec((qr, width), lambda i, idx: (idx[0], 0)),
    ]
    args = [og, gf]
    for m in moved:
        in_specs.append(pl.BlockSpec((tile, width), lambda i, idx: (i, 0)))
        in_specs.append(pl.BlockSpec((qr, width), lambda i, idx: (first, 0)))
        args += [m, m]
    for act in (mine, other):
        in_specs.append(pl.BlockSpec((4, act.shape[1], tile), lambda i, idx: (0, 0, i)))
        args.append(act)
    queries = qr // ranks
    return pl.pallas_call(
        functools.partial(score_kernel, ranks=ranks),
        grid_spec=pltpu.PrefetchScalarGridSpec(
            num_scalar_prefetch=1,
            grid=(tokens // tile,),
            in_specs=in_specs,
            out_specs=pl.BlockSpec((queries, tile), lambda i, idx: (0, i)),
        ),
        out_shape=jax.ShapeDtypeStruct((queries, tokens), F32),
        compiler_params=params(24 * MIB),
        cost_estimate=cost(2 * qr * tokens * width * 4, 4 * tokens * (qr + 4 * width)),
        name="scores",
    )(idx, *args)


def body(activations, down_weight, output_grads, act_factors, grad_factors, rank_weight):
    tokens = activations.shape[0]
    queries, ranks, hidden = act_factors.shape
    pipe, tensor = lax.axis_index("pipe"), lax.axis_index("tensor")
    x, core, y, z = pipe // 2, pipe % 2, tensor // 2, tensor % 2
    idx = jnp.stack([x, core, y, z]).astype(jnp.int32)

    gf = grad_factors.reshape(-1, grad_factors.shape[2])
    packed = pack(idx, output_grads, gf)
    moved = [
        lax.ppermute(p, "pipe", x_shift(d)) for p, d in zip(packed, (1, -1, 2))
    ]

    pieces = act_pieces(idx, act_factors.reshape(queries * ranks, hidden), activations)
    got = [lax.ppermute(pieces[j], "tensor", y_shift(j)) for j in (1, 3, 2)]
    own = (pieces[0] + got[2]) + (got[0] + got[1])
    own = own + lax.ppermute(own, "tensor", z_swap())
    weights = (rank_weight * (1.0 / math.sqrt(ranks))).reshape(4, -1)
    own = own * lax.dynamic_index_in_dim(weights, y, 0, keepdims=False)[:, None]
    mine = jnp.stack(
        [own] + [lax.ppermute(own, "tensor", y_shift(-j)) for j in (1, 2, 3)]
    )
    other = lax.ppermute(mine, "pipe", core_swap())

    outputs = []
    for block in range(2):
        keep, send = layer_z_first(idx, activations, down_weight, block, 384)
        total = keep + lax.ppermute(send, "tensor", z_swap())
        got = [lax.ppermute(total[j], "tensor", y_shift(j)) for j in (1, 3, 2)]
        total = (total[0] + got[2]) + (got[0] + got[1])
        outputs.append(total.astype(jnp.bfloat16))
    parts = layer_y_first(idx, activations, down_weight, 3, 256)
    got = [lax.ppermute(parts[j], "tensor", y_shift(j)) for j in (1, 3, 2)]
    total = (parts[0] + got[2]) + (got[0] + got[1])
    half = total.shape[1] // 2
    send = lax.dynamic_slice_in_dim(total, (1 - z) * half, half, 1)
    keep = lax.dynamic_slice_in_dim(total, z * half, half, 1)
    total = keep + lax.ppermute(send, "tensor", z_swap())
    outputs.append(total.astype(jnp.bfloat16))
    layer_output = jnp.concatenate(outputs, axis=0)

    share = scores(idx, output_grads, gf, moved, mine, other, ranks)
    raw = lax.dynamic_slice_in_dim(share, core * queries, queries, 0)
    send = lax.dynamic_slice_in_dim(share, (1 - core) * queries, queries, 0)
    raw = raw + lax.ppermute(send, "pipe", core_swap())
    got = [lax.ppermute(raw, "tensor", y_shift(j)) for j in (1, 3, 2)]
    raw = (raw + got[2]) + (got[0] + got[1])
    raw = raw + lax.ppermute(raw, "tensor", z_swap())

    square = jnp.sum((raw * raw).reshape(queries, -1, 128), axis=1)
    got = [lax.ppermute(square, "dp", dp_shift(j)) for j in (1, 3, 2)]
    square = (square + got[2]) + (got[0] + got[1])
    spread = jnp.sum(square, axis=1, keepdims=True) / (tokens * lax.axis_size("dp"))
    influence = raw / jnp.sqrt(spread + 1e-06)
    return (layer_output, influence.T)


def solution(mesh):
    return jax.shard_map(
        body,
        mesh=mesh,
        in_specs=(
            P("dp", "tensor"),
            P("tensor", "pipe"),
            P("dp", ("pipe", "tensor")),
            P("pipe", None, "tensor"),
            P(None, None, ("pipe", "tensor")),
            P("pipe", None),
        ),
        out_specs=(P("dp", ("pipe", "tensor")), P("dp", "pipe")),
        check_vma=False,
    )
```

```python
import functools
import math

import jax
import jax.numpy as jnp
from jax import lax
from jax.experimental import pallas as pl
from jax.experimental.pallas import tpu as pltpu
from jax.sharding import PartitionSpec as P

F32 = jnp.float32
MIB = 1 << 20


def x_shift(d):
    return [(p, ((p // 2 + d) % 4) * 2 + p % 2) for p in range(8)]


def core_swap():
    return [(p, p ^ 1) for p in range(8)]


def y_shift(d):
    return [(t, ((t // 2 + d) % 4) * 2 + t % 2) for t in range(8)]


def z_swap():
    return [(t, t ^ 1) for t in range(8)]


def dp_shift(d):
    return [(i, (i + d) % 4) for i in range(4)]


def params(limit):
    return pltpu.CompilerParams(vmem_limit_bytes=limit)


def cost():
    return pl.CostEstimate(flops=0, bytes_accessed=0, transcendentals=0)


def after(value, *others):
    return lax.optimization_barrier((value, *others))[0]


def pack_kernel(idx, og, gf, fwd, bwd):
    half = og.shape[0] // 2
    rows = gf.shape[0] // 4

    def gf_rows(d, first, count):
        start = lax.rem(idx[0] + d, 4) * rows + first
        return gf[pl.ds(pl.multiple_of(start, count), count), :].astype(F32)

    low, high = og[:half, :].astype(F32), og[half:, :].astype(F32)
    for out, d, ahead, behind, part in ((fwd, 1, high, low, 0), (bwd, 3, low, high, 1)):
        out[:half, :] = ahead
        out[half : half + rows, :] = gf_rows(d, 0, rows)
        out[half + rows : 2 * half + rows, :] = behind
        out[2 * half + rows :, :] = gf_rows(2, part * (rows // 2), rows // 2)


def pack(idx, og, gf):
    tokens, width = og.shape
    rows = tokens + gf.shape[0] // 4 * 3 // 2
    whole = pl.BlockSpec(memory_space=pltpu.VMEM)
    return pl.pallas_call(
        pack_kernel,
        grid_spec=pltpu.PrefetchScalarGridSpec(
            num_scalar_prefetch=1, grid=(), in_specs=[whole, whole], out_specs=[whole] * 2
        ),
        out_shape=[jax.ShapeDtypeStruct((rows, width), F32)] * 2,
        compiler_params=params(16 * MIB),
        cost_estimate=cost(),
        name="pack",
    )(idx, og, gf)


def act_kernel(idx, af, a, *rest):
    *outs, scratch = rest
    scratch[...] = lax.dot_general(
        af[...], a[...], (((1,), (1,)), ((), ())), preferred_element_type=F32
    )
    rows = outs[0].shape[0]
    for j, out in enumerate(outs):
        start = pl.multiple_of(lax.rem(idx[2] + j, 4) * rows, rows)
        out[...] = scratch[pl.ds(start, rows), :]


def act_pieces(idx, af, a):
    qr, hidden = af.shape
    tokens = a.shape[0]
    tile = 256
    return pl.pallas_call(
        act_kernel,
        grid_spec=pltpu.PrefetchScalarGridSpec(
            num_scalar_prefetch=1,
            grid=(tokens // tile,),
            in_specs=[
                pl.BlockSpec((qr, hidden), lambda i, idx: (0, 0)),
                pl.BlockSpec((tile, hidden), lambda i, idx: (i, 0)),
            ],
            out_specs=[pl.BlockSpec((qr // 4, tile), lambda i, idx: (0, i))] * 4,
            scratch_shapes=[pltpu.VMEM((qr, tile), F32)],
        ),
        out_shape=[jax.ShapeDtypeStruct((qr // 4, tokens), F32)] * 4,
        compiler_params=params(24 * MIB),
        cost_estimate=cost(),
        name="act",
    )(idx, af, a)


def layer_z_kernel(idx, a, w, keep, send):
    acc = jnp.dot(a[...], w[...], preferred_element_type=F32)
    half = acc.shape[1] // 2

    @pl.when(idx[3] == 0)
    def _():
        keep[0] = acc[:, :half]
        send[0] = acc[:, half:]

    @pl.when(idx[3] == 1)
    def _():
        keep[0] = acc[:, half:]
        send[0] = acc[:, :half]


def layer_z_first(idx, a, w, block, rows):
    hidden, cols = w.shape
    width = cols // 4
    return pl.pallas_call(
        layer_z_kernel,
        grid_spec=pltpu.PrefetchScalarGridSpec(
            num_scalar_prefetch=1,
            grid=(4,),
            in_specs=[
                pl.BlockSpec((rows, hidden), lambda j, idx: (block, 0)),
                pl.BlockSpec((hidden, width), lambda j, idx: (0, lax.rem(idx[2] + j, 4))),
            ],
            out_specs=[pl.BlockSpec((1, rows, width // 2), lambda j, idx: (j, 0, 0))] * 2,
        ),
        out_shape=[jax.ShapeDtypeStruct((4, rows, width // 2), F32)] * 2,
        compiler_params=params(24 * MIB),
        cost_estimate=cost(),
        name="layer_z",
    )(idx, a, w)


def layer_y_kernel(idx, a, w, *outs):
    for j, out in enumerate(outs):

        @pl.when(pl.program_id(0) == j)
        def _(out=out):
            out[...] = jnp.dot(a[...], w[...], preferred_element_type=F32)


def layer_y_first(idx, a, w, block, rows):
    hidden, cols = w.shape
    width = cols // 4
    return pl.pallas_call(
        layer_y_kernel,
        grid_spec=pltpu.PrefetchScalarGridSpec(
            num_scalar_prefetch=1,
            grid=(4,),
            in_specs=[
                pl.BlockSpec((rows, hidden), lambda j, idx: (block, 0)),
                pl.BlockSpec((hidden, width), lambda j, idx: (0, lax.rem(idx[2] + j, 4))),
            ],
            out_specs=[pl.BlockSpec((rows, width), lambda j, idx: (0, 0))] * 4,
        ),
        out_shape=[jax.ShapeDtypeStruct((rows, width), F32)] * 4,
        compiler_params=params(24 * MIB),
        cost_estimate=cost(),
        name="layer_y",
    )(idx, a, w)


def score_kernel(
    idx, og, gf, a1, b1, a3, b3, a2, b2, a2_, b2_, mine, other, out, *, ranks
):
    bf = jnp.bfloat16
    far = jnp.where(pl.program_id(0) < pl.num_programs(0) // 2, a2[...], a2_[...])
    far_rows = jnp.concatenate([b2[...], b2_[...]], axis=0)
    lhs = jnp.concatenate(
        [gf[...]] + [b.astype(bf) for b in (b1[...], b3[...], far_rows)], axis=1
    )
    rhs = jnp.concatenate([og[...]] + [a.astype(bf) for a in (a1[...], a3[...], far)], axis=1)
    grad = lax.dot_general(lhs, rhs, (((1,), (1,)), ((), ())), preferred_element_type=F32)
    rows = mine.shape[1]
    parts = []
    for c in range(2):
        for b in range(4):
            j = lax.rem(b + 4 - idx[2], 4)
            act = jnp.where(idx[1] == c, mine[j], other[j])
            at = (c * 4 + b) * rows
            product = grad[at : at + rows, :] * act
            for q in range(rows // ranks):
                parts.append(
                    jnp.sum(product[q * ranks : (q + 1) * ranks], axis=0, keepdims=True)
                )
    out[...] = jnp.concatenate(parts, axis=0)


def scores(idx, og, gf, near, far, mine, other, ranks):
    tokens, width = og.shape
    qr = gf.shape[0] // 4
    steps = 4
    tile = tokens // steps
    mid = steps // 2
    assert tokens == 2 * qr
    spec = lambda rows, at: pl.BlockSpec((rows, width), lambda i, idx: (at(i, idx), 0))
    in_specs = [
        spec(tile, lambda i, idx: i),
        spec(qr, lambda i, idx: idx[0]),
        spec(tile, lambda i, idx: jnp.where(i < mid, i + 2 * mid, i - mid)),
        spec(qr, lambda i, idx: 1),
        spec(tile, lambda i, idx: jnp.where(i < mid, i, i + mid)),
        spec(qr, lambda i, idx: 1),
        spec(tile, lambda i, idx: jnp.minimum(i, mid - 1)),
        spec(qr // 2, lambda i, idx: 2),
        spec(tile, lambda i, idx: jnp.maximum(i - mid, 0)),
        spec(qr // 2, lambda i, idx: 2),
    ]
    args = [og, gf, near[0], near[0], near[1], near[1], far[0], far[0], far[1], far[1]]
    for act in (mine, other):
        in_specs.append(pl.BlockSpec((4, act.shape[1], tile), lambda i, idx: (0, 0, i)))
        args.append(act)
    queries = qr // ranks
    return pl.pallas_call(
        functools.partial(score_kernel, ranks=ranks),
        grid_spec=pltpu.PrefetchScalarGridSpec(
            num_scalar_prefetch=1,
            grid=(steps,),
            in_specs=in_specs,
            out_specs=pl.BlockSpec((queries, tile), lambda i, idx: (0, i)),
        ),
        out_shape=jax.ShapeDtypeStruct((queries, tokens), F32),
        compiler_params=params(24 * MIB),
        cost_estimate=cost(),
        name="scores",
    )(idx, *args)


def along_y(parts, shifts=(1, 3, 2)):
    got = [lax.ppermute(parts[j], "tensor", y_shift(j)) for j in shifts]
    return (parts[0] + got[2]) + (got[0] + got[1])


def body(activations, down_weight, output_grads, act_factors, grad_factors, rank_weight):
    tokens = activations.shape[0]
    queries, ranks, hidden = act_factors.shape
    pipe, tensor = lax.axis_index("pipe"), lax.axis_index("tensor")
    x, core, y, z = pipe // 2, pipe % 2, tensor // 2, tensor % 2
    idx = jnp.stack([x, core, y, z]).astype(jnp.int32)
    act_factors = act_factors.reshape(queries * ranks, hidden)
    activations, down_weight, act_factors = (
        pltpu.with_memory_space_constraint(v, pltpu.HBM)
        for v in (activations, down_weight, act_factors)
    )

    gf = grad_factors.reshape(-1, grad_factors.shape[2])
    fwd, bwd = pack(idx, output_grads, gf)
    near = [lax.ppermute(fwd, "pipe", x_shift(1)), lax.ppermute(bwd, "pipe", x_shift(-1))]

    at = after(idx, fwd)
    pieces = act_pieces(at, act_factors, activations)
    own = along_y(pieces)

    at = after(idx, pieces[0])
    keep0, send0 = layer_z_first(at, activations, down_weight, 0, 384)
    got0 = lax.ppermute(send0, "tensor", z_swap())
    at = after(idx, keep0)
    parts = layer_y_first(at, activations, down_weight, 3, 256)
    wide = along_y(parts)
    at = after(idx, parts[0])
    keep1, send1 = layer_z_first(at, activations, down_weight, 1, 384)

    own, near[0], near[1] = lax.optimization_barrier((own, near[0], near[1]))
    at = near[0].shape[0] - tokens // 2 - gf.shape[0] // 8
    far = [
        lax.ppermute(near[0][at:], "pipe", x_shift(1)),
        lax.ppermute(near[1][at:], "pipe", x_shift(-1)),
    ]
    own = own + lax.ppermute(own, "tensor", z_swap())
    got1 = lax.ppermute(send1, "tensor", z_swap())
    weights = (rank_weight * (1.0 / math.sqrt(ranks))).reshape(4, -1)
    own = own * lax.dynamic_index_in_dim(weights, y, 0, keepdims=False)[:, None]

    own, got0, wide, keep1 = lax.optimization_barrier((own, got0, wide, keep1))
    mine = jnp.stack(
        [own] + [lax.ppermute(own, "tensor", y_shift(-j)) for j in (1, 2, 3)]
    )
    mine, far[0], far[1], got1 = lax.optimization_barrier((mine, far[0], far[1], got1))
    other = lax.ppermute(mine, "pipe", core_swap())

    half = wide.shape[1] // 2
    send = lax.dynamic_slice_in_dim(wide, (1 - z) * half, half, 1)
    keep = lax.dynamic_slice_in_dim(wide, z * half, half, 1)
    out2 = (keep + lax.ppermute(send, "tensor", z_swap())).astype(jnp.bfloat16)
    out0 = along_y(keep0 + got0).astype(jnp.bfloat16)
    out1 = along_y(keep1 + got1).astype(jnp.bfloat16)

    share = scores(idx, output_grads, gf, near, far, mine, other, ranks)
    raw = lax.dynamic_slice_in_dim(share, core * queries, queries, 0)
    send = lax.dynamic_slice_in_dim(share, (1 - core) * queries, queries, 0)
    raw = raw + lax.ppermute(send, "pipe", core_swap())
    raw = along_y([raw] * 4)
    raw = raw + lax.ppermute(raw, "tensor", z_swap())

    square = jnp.sum((raw * raw).reshape(queries, -1, 128), axis=1)
    got = [lax.ppermute(square, "dp", dp_shift(j)) for j in (1, 3, 2)]
    square = (square + got[2]) + (got[0] + got[1])
    spread = jnp.sum(square, axis=1, keepdims=True) / (tokens * lax.axis_size("dp"))
    influence = raw / jnp.sqrt(spread + 1e-06)
    return (jnp.concatenate([out0, out1, out2], axis=0), influence.T)


def solution(mesh):
    return jax.shard_map(
        body,
        mesh=mesh,
        in_specs=(
            P("dp", "tensor"),
            P("tensor", "pipe"),
            P("dp", ("pipe", "tensor")),
            P("pipe", None, "tensor"),
            P(None, None, ("pipe", "tensor")),
            P("pipe", None),
        ),
        out_specs=(P("dp", ("pipe", "tensor")), P("dp", "pipe")),
        check_vma=False,
    )
```

```python
import functools
import math

import jax
import jax.numpy as jnp
from jax import lax
from jax.experimental import pallas as pl
from jax.experimental.pallas import tpu as pltpu
from jax.sharding import PartitionSpec as P

F32 = jnp.float32
MIB = 1 << 20
WHOLE = pl.BlockSpec(memory_space=pltpu.VMEM)


def x_ring():
    return [(p, ((p // 2 + 1 - 2 * (p % 2)) % 4) * 2 + p % 2) for p in range(8)]


def core_swap():
    return [(p, p ^ 1) for p in range(8)]


def y_shift(d):
    return [(t, ((t // 2 + d) % 4) * 2 + t % 2) for t in range(8)]


def z_swap():
    return [(t, t ^ 1) for t in range(8)]


def dp_shift(d):
    return [(i, (i + d) % 4) for i in range(4)]


def params(limit):
    return pltpu.CompilerParams(vmem_limit_bytes=limit)


def cost():
    return pl.CostEstimate(flops=0, bytes_accessed=0, transcendentals=0)


def in_hbm(value):
    return pltpu.with_memory_space_constraint(value, pltpu.HBM)


def in_vmem(value):
    return pltpu.with_memory_space_constraint(value, pltpu.VMEM)


def after(value, *others):
    return lax.optimization_barrier((value, *others))[0]


def pack_kernel(idx, og_hbm, gf_hbm, mine, other, og, gf, sems):
    copies = [
        pltpu.make_async_copy(src, dst, sems.at[i])
        for i, (src, dst) in enumerate(((og_hbm, og), (gf_hbm, gf)))
    ]
    for copy in copies:
        copy.start()
    tokens = og.shape[0]
    rows = gf.shape[0] // 4

    def gf_rows(distance):
        start = lax.rem(idx[0] + distance, 4) * rows
        return gf[pl.ds(pl.multiple_of(start, rows), rows), :].astype(F32)

    copies[0].wait()
    wide = og[...].astype(F32)
    other[rows : rows + tokens, :] = wide
    mine[rows : rows + tokens, :] = wide
    copies[1].wait()
    other[:rows, :] = gf_rows(3 - 2 * idx[1])
    mine[:rows, :] = gf_rows(1 + 2 * idx[1])
    mine[rows + tokens :, :] = gf_rows(2)


def pack(idx, og, gf):
    tokens, width = og.shape
    rows = gf.shape[0] // 4
    return pl.pallas_call(
        pack_kernel,
        grid_spec=pltpu.PrefetchScalarGridSpec(
            num_scalar_prefetch=1,
            grid=(),
            in_specs=[pl.BlockSpec(memory_space=pltpu.HBM)] * 2,
            out_specs=[WHOLE] * 2,
            scratch_shapes=[
                pltpu.VMEM(og.shape, og.dtype),
                pltpu.VMEM(gf.shape, gf.dtype),
                pltpu.SemaphoreType.DMA((2,)),
            ],
        ),
        out_shape=[
            jax.ShapeDtypeStruct((r, width), F32) for r in (tokens + 2 * rows, tokens + rows)
        ],
        compiler_params=params(16 * MIB),
        cost_estimate=cost(),
        name="pack",
    )(idx, in_hbm(og), in_hbm(gf))


def act_kernel(idx, af_hbm, a_hbm, out0, out1, out2, out3, a, af, scratch, sems):
    outs = (out0, out1, out2, out3)
    rows = out0.shape[0]
    tile = scratch.shape[1]
    steps = a.shape[0] // tile

    def rows_of(i):
        return pl.ds(i * tile, tile)

    copies = [pltpu.make_async_copy(af_hbm, af, sems.at[steps])] + [
        pltpu.make_async_copy(a_hbm.at[rows_of(i), :], a.at[rows_of(i), :], sems.at[i])
        for i in range(steps)
    ]
    for copy in copies:
        copy.start()
    copies[0].wait()
    for i in range(steps):
        copies[1 + i].wait()
        scratch[...] = lax.dot_general(
            af[...], a[rows_of(i), :], (((1,), (1,)), ((), ())), preferred_element_type=F32
        )
        for j, out in enumerate(outs):
            start = pl.multiple_of(lax.rem(idx[2] + j, 4) * rows, rows)
            out[:, rows_of(i)] = scratch[pl.ds(start, rows), :]


def act_pieces(idx, af, a):
    qr, tokens = af.shape[0], a.shape[0]
    steps = 4
    return pl.pallas_call(
        act_kernel,
        grid_spec=pltpu.PrefetchScalarGridSpec(
            num_scalar_prefetch=1,
            grid=(),
            in_specs=[pl.BlockSpec(memory_space=pltpu.HBM)] * 2,
            out_specs=[WHOLE] * 5,
            scratch_shapes=[
                pltpu.VMEM(af.shape, af.dtype),
                pltpu.VMEM((qr, tokens // steps), F32),
                pltpu.SemaphoreType.DMA((steps + 1,)),
            ],
        ),
        out_shape=[jax.ShapeDtypeStruct((qr // 4, tokens), F32)] * 4
        + [jax.ShapeDtypeStruct(a.shape, a.dtype)],
        compiler_params=params(24 * MIB),
        cost_estimate=cost(),
        name="act",
    )(idx, in_hbm(af), in_hbm(a))


def layer_z_kernel(idx, a, w_in, keep, send, *rest, first, relative):
    rows, half = keep.shape[1:]
    width = 2 * half

    def columns(j):
        owner = lax.rem(idx[2] + j, 4) if relative else j
        return pl.ds(pl.multiple_of(owner * width, width), width)

    def step(j, w):
        acc = jnp.dot(
            a[first : first + rows, :], w[:, columns(j)], preferred_element_type=F32
        )
        low, high = acc[:, :half], acc[:, half:]
        at_low = idx[3] == 0
        keep[j] = jnp.where(at_low, low, high)
        send[j] = jnp.where(at_low, high, low)

    if rest:
        w, sems = rest
        copies = [
            pltpu.make_async_copy(w_in.at[:, columns(j)], w.at[:, columns(j)], sems.at[j])
            for j in range(4)
        ]
        for copy in copies:
            copy.start()
        for j in range(4):
            copies[j].wait()
            step(j, w)
    else:
        pl.loop(0, 4)(lambda j: step(j, w_in))


def layer_z_first(idx, a, w, first, rows, relative, load=False):
    shape = jax.ShapeDtypeStruct((4, rows, w.shape[1] // 8), F32)
    return pl.pallas_call(
        functools.partial(layer_z_kernel, first=first, relative=relative),
        grid_spec=pltpu.PrefetchScalarGridSpec(
            num_scalar_prefetch=1,
            grid=(),
            in_specs=[WHOLE, pl.BlockSpec(memory_space=pltpu.HBM) if load else WHOLE],
            out_specs=[WHOLE] * (2 + load),
            scratch_shapes=[pltpu.SemaphoreType.DMA((4,))] * load,
        ),
        out_shape=[shape] * 2 + [jax.ShapeDtypeStruct(w.shape, w.dtype)] * load,
        compiler_params=params(24 * MIB),
        cost_estimate=cost(),
        name="layer_z",
    )(idx, in_vmem(a), in_hbm(w) if load else in_vmem(w))


def layer_y_kernel(idx, a, w, out, *, first):
    _, rows, width = out.shape

    @pl.loop(0, 4)
    def _(j):
        start = pl.multiple_of(j * width, width)
        out[j] = jnp.dot(
            a[first : first + rows, :], w[:, pl.ds(start, width)], preferred_element_type=F32
        )


def layer_y_first(idx, a, w, first, rows):
    return pl.pallas_call(
        functools.partial(layer_y_kernel, first=first),
        grid_spec=pltpu.PrefetchScalarGridSpec(
            num_scalar_prefetch=1, grid=(), in_specs=[WHOLE] * 2, out_specs=WHOLE
        ),
        out_shape=jax.ShapeDtypeStruct((4, rows, w.shape[1] // 4), F32),
        compiler_params=params(24 * MIB),
        cost_estimate=cost(),
        name="layer_y",
    )(idx, in_vmem(a), in_vmem(w))


def score_kernel(idx, og, gf, a1, b1, a2, b2, a3, b3, mine, other, out, *, ranks):
    bf = jnp.bfloat16
    lhs = jnp.concatenate([gf[...]] + [b[...].astype(bf) for b in (b1, b2, b3)], axis=1)
    rhs = jnp.concatenate([og[...]] + [a[...].astype(bf) for a in (a1, a2, a3)], axis=1)
    grad = lax.dot_general(lhs, rhs, (((1,), (1,)), ((), ())), preferred_element_type=F32)
    rows = mine.shape[1]
    parts = []
    for c in range(2):
        for b in range(4):
            j = lax.rem(b + 4 - idx[2], 4)
            act = jnp.where(idx[1] == c, mine[j], other[j])
            at = (c * 4 + b) * rows
            product = grad[at : at + rows, :] * act
            for q in range(0, rows, ranks):
                parts.append(jnp.sum(product[q : q + ranks], axis=0, keepdims=True))
    out[...] = jnp.concatenate(parts, axis=0)


def scores(idx, og, gf, near, far, mine, other, ranks):
    tokens, width = og.shape
    qr = gf.shape[0] // 4
    tile = 256
    assert qr % tile == 0 and tokens % qr == 0
    spec = lambda rows, at: pl.BlockSpec((rows, width), lambda i, idx: (at(i, idx), 0))
    skip, step = qr // tile, (tokens + 2 * qr) // tile
    in_specs = [
        spec(tile, lambda i, idx: i),
        spec(qr, lambda i, idx: idx[0]),
        spec(tile, lambda i, idx: skip + i),
        spec(qr, lambda i, idx: 0),
        spec(tile, lambda i, idx: step + skip + i),
        spec(qr, lambda i, idx: tokens // qr + 2),
        spec(tile, lambda i, idx: i),
        spec(qr, lambda i, idx: tokens // qr),
    ]
    args = [og, gf, near, near, near, near, far, far]
    for act in (mine, other):
        in_specs.append(pl.BlockSpec((4, act.shape[1], tile), lambda i, idx: (0, 0, i)))
        args.append(act)
    return pl.pallas_call(
        functools.partial(score_kernel, ranks=ranks),
        grid_spec=pltpu.PrefetchScalarGridSpec(
            num_scalar_prefetch=1,
            grid=(tokens // tile,),
            in_specs=in_specs,
            out_specs=pl.BlockSpec((qr // ranks, tile), lambda i, idx: (0, i)),
        ),
        out_shape=jax.ShapeDtypeStruct((qr // ranks, tokens), F32),
        compiler_params=params(24 * MIB),
        cost_estimate=cost(),
        name="scores",
    )(idx, *args)


def along_y(parts, shifts=(1, 3, 2)):
    got = [lax.ppermute(parts[j], "tensor", y_shift(j)) for j in shifts]
    return (parts[0] + got[2]) + (got[0] + got[1])


def scatter_y(parts):
    groups = [[2 * i + z for i in range(4)] for z in range(2)]
    return lax.psum_scatter(parts, "tensor", scatter_dimension=0, axis_index_groups=groups)


def body(activations, down_weight, output_grads, act_factors, grad_factors, rank_weight):
    tokens = activations.shape[0]
    queries, ranks, hidden = act_factors.shape
    pipe, tensor = lax.axis_index("pipe"), lax.axis_index("tensor")
    x, core, y, z = pipe // 2, pipe % 2, tensor // 2, tensor % 2
    idx = jnp.stack([x, core, y, z]).astype(jnp.int32)
    gf = grad_factors.reshape(-1, grad_factors.shape[2])

    swap = functools.partial(lax.ppermute, axis_name="pipe", perm=core_swap())
    ring = functools.partial(lax.ppermute, axis_name="pipe", perm=x_ring())
    packed, other = pack(idx, output_grads, gf)
    got = swap(other)
    at = after(idx, packed)
    *pieces, held = act_pieces(at, act_factors.reshape(queries * ranks, hidden), activations)
    own = along_y(pieces)

    got, pieces[0] = lax.optimization_barrier((got, pieces[0]))
    near = ring(jnp.concatenate([packed, got]))

    at = after(idx, pieces[0])
    keep0, send0, weight = layer_z_first(at, held, down_weight, 0, 192, True, load=True)
    got0 = lax.ppermute(send0, "tensor", z_swap())
    at = after(idx, keep0)
    parts = layer_y_first(at, held, weight, 768, 256)
    wide = scatter_y(parts)
    at = after(idx, parts)
    keep1, send1 = layer_z_first(at, held, weight, 192, 320, True)
    at = after(idx, keep1)
    keep2, send2 = layer_z_first(at, held, weight, 512, 256, True)

    own, keep1, keep2 = lax.optimization_barrier((own, keep1, keep2))
    own = own + lax.ppermute(own, "tensor", z_swap())
    weights = (rank_weight * (1.0 / math.sqrt(ranks))).reshape(4, -1)
    own = own * lax.dynamic_index_in_dim(weights, y, 0, keepdims=False)[:, None]

    own, near, send1, got0 = lax.optimization_barrier((own, near, send1, got0))
    far = ring(near[gf.shape[0] // 4 : packed.shape[0]])
    got1 = lax.ppermute(send1, "tensor", z_swap())
    mine = jnp.stack(
        [own] + [lax.ppermute(own, "tensor", y_shift(-j)) for j in (1, 2, 3)]
    )
    mine, far, got1, wide = lax.optimization_barrier((mine, far, got1, wide))
    other = swap(mine)
    out0 = along_y(jnp.concatenate([keep0 + got0, keep1 + got1], axis=1))
    out0 = out0.astype(jnp.bfloat16)
    got2 = lax.ppermute(send2, "tensor", z_swap())

    share = scores(idx, output_grads, gf, near, far, mine, other, ranks)
    raw = lax.dynamic_slice_in_dim(share, core * queries, queries, 0)
    raw = raw + swap(lax.dynamic_slice_in_dim(share, (1 - core) * queries, queries, 0))
    raw = along_y([raw] * 4)
    raw, got2, out0 = lax.optimization_barrier((raw, got2, out0))
    half = keep0.shape[2]
    send = lax.dynamic_slice_in_dim(wide, (1 - z) * half, half, 1)
    keep = lax.dynamic_slice_in_dim(wide, z * half, half, 1)
    out2 = (keep + lax.ppermute(send, "tensor", z_swap())).astype(jnp.bfloat16)
    out1 = along_y(keep2 + got2).astype(jnp.bfloat16)
    raw = raw + lax.ppermute(raw, "tensor", z_swap())

    square = jnp.sum((raw * raw).reshape(queries, -1, 128), axis=1)
    got = [lax.ppermute(square, "dp", dp_shift(j)) for j in (1, 3, 2)]
    square = (square + got[2]) + (got[0] + got[1])
    square, out1 = lax.optimization_barrier((square, out1))
    spread = jnp.sum(square, axis=1, keepdims=True) / (tokens * lax.axis_size("dp"))
    influence = raw / jnp.sqrt(spread + 1e-06)
    return (jnp.concatenate([out0, out1, out2], axis=0), influence.T)


def solution(mesh):
    return jax.shard_map(
        body,
        mesh=mesh,
        in_specs=(
            P("dp", "tensor"),
            P("tensor", "pipe"),
            P("dp", ("pipe", "tensor")),
            P("pipe", None, "tensor"),
            P(None, None, ("pipe", "tensor")),
            P("pipe", None),
        ),
        out_specs=(P("dp", ("pipe", "tensor")), P("dp", "pipe")),
        check_vma=False,
    )
```

```python
import functools
import math

import jax
import jax.numpy as jnp
from jax import lax
from jax.experimental import pallas as pl
from jax.experimental.pallas import tpu as pltpu
from jax.sharding import PartitionSpec as P

F32 = jnp.float32
MIB = 1 << 20
WHOLE = pl.BlockSpec(memory_space=pltpu.VMEM)
PACK_COST = 40 * MIB
ACT_COST = 20 * MIB


def x_ring():
    return [(p, ((p // 2 + 1 - 2 * (p % 2)) % 4) * 2 + p % 2) for p in range(8)]


def core_swap():
    return [(p, p ^ 1) for p in range(8)]


def y_shift(d):
    return [(t, ((t // 2 + d) % 4) * 2 + t % 2) for t in range(8)]


def y_pair():
    return [(t, t ^ 2) for t in range(8)]


def z_swap():
    return [(t, t ^ 1) for t in range(8)]


def dp_shift(d):
    return [(i, (i + d) % 4) for i in range(4)]


def params(limit):
    return pltpu.CompilerParams(vmem_limit_bytes=limit)


def cost(nbytes=0):
    return pl.CostEstimate(flops=0, bytes_accessed=nbytes, transcendentals=0)


def in_hbm(value):
    return pltpu.with_memory_space_constraint(value, pltpu.HBM)


def in_vmem(value):
    return pltpu.with_memory_space_constraint(value, pltpu.VMEM)


def after(value, *others):
    return lax.optimization_barrier((value, *others))[0]


def pack_kernel(idx, og_hbm, gf_hbm, *refs):
    *hbm, mine, other, a, af, weight, og, gf, sems = refs
    held = (a, af, weight)
    copies = [
        pltpu.make_async_copy(src, dst, sems.at[i])
        for i, (src, dst) in enumerate(((og_hbm, og), (gf_hbm, gf), *zip(hbm, held)))
    ]
    for copy in copies:
        copy.start()
    tokens = og.shape[0]
    rows = gf.shape[0] // 4

    def gf_rows(distance):
        start = lax.rem(idx[0] + distance, 4) * rows
        return gf[pl.ds(pl.multiple_of(start, rows), rows), :].astype(F32)

    copies[0].wait()
    wide = og[...].astype(F32)
    other[rows : rows + tokens, :] = wide
    mine[rows : rows + tokens, :] = wide
    copies[1].wait()
    other[:rows, :] = gf_rows(3 - 2 * idx[1])
    mine[:rows, :] = gf_rows(1 + 2 * idx[1])
    mine[rows + tokens :, :] = gf_rows(2)
    for copy in copies[2:]:
        copy.wait()


def pack(idx, og, gf, held):
    tokens, width = og.shape
    rows = gf.shape[0] // 4
    return pl.pallas_call(
        pack_kernel,
        grid_spec=pltpu.PrefetchScalarGridSpec(
            num_scalar_prefetch=1,
            grid=(),
            in_specs=[pl.BlockSpec(memory_space=pltpu.HBM)] * (2 + len(held)),
            out_specs=[WHOLE] * (2 + len(held)),
            scratch_shapes=[
                pltpu.VMEM(og.shape, og.dtype),
                pltpu.VMEM(gf.shape, gf.dtype),
                pltpu.SemaphoreType.DMA((2 + len(held),)),
            ],
        ),
        out_shape=[
            jax.ShapeDtypeStruct((r, width), F32) for r in (tokens + 2 * rows, tokens + rows)
        ]
        + [jax.ShapeDtypeStruct(v.shape, v.dtype) for v in held],
        compiler_params=params(4 * MIB),
        cost_estimate=cost(PACK_COST),
        name="pack",
    )(idx, *map(in_hbm, (og, gf, *held)))


def act_kernel(idx, weight, af, a, out0, out1, out2, out3, scratch, *, scale):
    rows = out0.shape[0]
    tile = scratch.shape[1]
    queries, ranks = weight.shape
    diagonal = lax.broadcasted_iota(jnp.int32, (ranks, ranks), 0) == lax.broadcasted_iota(
        jnp.int32, (ranks, ranks), 1
    )
    column = jnp.concatenate(
        [
            jnp.sum(
                jnp.where(diagonal, weight[q : q + 1, :] * scale, 0.0), axis=1, keepdims=True
            )
            for q in range(queries)
        ],
        axis=0,
    )

    @pl.loop(0, a.shape[0] // tile)
    def _(i):
        at = pl.ds(pl.multiple_of(i * tile, tile), tile)
        scratch[...] = column * lax.dot_general(
            af[...], a[at, :], (((1,), (1,)), ((), ())), preferred_element_type=F32
        )
        for j, out in enumerate((out0, out1, out2, out3)):
            start = pl.multiple_of(lax.rem(idx[2] + j, 4) * rows, rows)
            out[:, at] = scratch[pl.ds(start, rows), :]


def act_pieces(idx, weight, af, a):
    qr, tokens = af.shape[0], a.shape[0]
    return pl.pallas_call(
        functools.partial(act_kernel, scale=1.0 / math.sqrt(weight.shape[1])),
        grid_spec=pltpu.PrefetchScalarGridSpec(
            num_scalar_prefetch=1,
            grid=(),
            in_specs=[WHOLE] * 3,
            out_specs=[WHOLE] * 4,
            scratch_shapes=[pltpu.VMEM((qr, 256), F32)],
        ),
        out_shape=[jax.ShapeDtypeStruct((qr // 4, tokens), F32)] * 4,
        compiler_params=params(8 * MIB),
        cost_estimate=cost(ACT_COST),
        name="act",
    )(idx, weight, in_vmem(af), in_vmem(a))


def layer_kernel(idx, a, w, *outs, first, blocks):
    width = w.shape[1] // 4

    @pl.loop(0, 4)
    def _(j):
        owner = lax.rem(idx[2] + j, 4)
        acc = jnp.dot(
            a[first : first + sum(blocks), :],
            w[:, pl.ds(pl.multiple_of(owner * width, width), width)],
            preferred_element_type=F32,
        )
        low, high = acc[:, : width // 2], acc[:, width // 2 :]
        at_low = idx[3] == 0
        at = 0
        for rows, keep, send in zip(blocks, outs[0::2], outs[1::2]):
            keep[j] = jnp.where(at_low, low[at : at + rows], high[at : at + rows])
            send[j] = jnp.where(at_low, high[at : at + rows], low[at : at + rows])
            at += rows


def layer(idx, a, w, first, blocks):
    shapes = [
        jax.ShapeDtypeStruct((4, rows, w.shape[1] // 8), F32) for rows in blocks for _ in range(2)
    ]
    return pl.pallas_call(
        functools.partial(layer_kernel, first=first, blocks=blocks),
        grid_spec=pltpu.PrefetchScalarGridSpec(
            num_scalar_prefetch=1,
            grid=(),
            in_specs=[WHOLE] * 2,
            out_specs=[WHOLE] * len(shapes),
        ),
        out_shape=shapes,
        compiler_params=params(8 * MIB),
        cost_estimate=cost(),
        name="layer",
    )(idx, in_vmem(a), in_vmem(w))


def score_kernel(idx, og, gf, a1, b1, a2, b2, a3, b3, mine, other, keep, send, *, ranks):
    bf = jnp.bfloat16
    lhs = jnp.concatenate([gf[...]] + [b[...].astype(bf) for b in (b1, b2, b3)], axis=1)
    rhs = jnp.concatenate([og[...]] + [a[...].astype(bf) for a in (a1, a2, a3)], axis=1)
    grad = lax.dot_general(lhs, rhs, (((1,), (1,)), ((), ())), preferred_element_type=F32)
    rows = mine.shape[1]
    sums = []
    for c in range(2):
        parts = []
        for b in range(4):
            j = lax.rem(b + 4 - idx[2], 4)
            act = jnp.where(idx[1] == c, mine[j], other[j])
            at = (c * 4 + b) * rows
            product = grad[at : at + rows, :] * act
            for q in range(0, rows, ranks):
                parts.append(jnp.sum(product[q : q + ranks], axis=0, keepdims=True))
        sums.append(jnp.concatenate(parts, axis=0))
    keep[...] = jnp.where(idx[1] == 0, sums[0], sums[1])
    send[...] = jnp.where(idx[1] == 0, sums[1], sums[0])


def scores(idx, og, gf, near, far, mine, other, ranks):
    tokens, width = og.shape
    qr = gf.shape[0] // 4
    tile = 256
    assert qr % tile == 0 and tokens % qr == 0
    spec = lambda rows, at: pl.BlockSpec((rows, width), lambda i, idx: (at(i, idx), 0))
    skip = qr // tile
    in_specs = [
        spec(tile, lambda i, idx: i),
        spec(qr, lambda i, idx: idx[0]),
        spec(tile, lambda i, idx: skip + i),
        spec(qr, lambda i, idx: 0),
        spec(tile, lambda i, idx: skip + i),
        spec(qr, lambda i, idx: 0),
        spec(tile, lambda i, idx: i),
        spec(qr, lambda i, idx: tokens // qr),
    ]
    args = [in_hbm(og), in_hbm(gf), near[0], near[0], near[1], near[1], far, far]
    for act in (mine, other):
        in_specs.append(pl.BlockSpec((4, act.shape[1], tile), lambda i, idx: (0, 0, i)))
        args.append(act)
    half = qr // ranks // 2
    return pl.pallas_call(
        functools.partial(score_kernel, ranks=ranks),
        grid_spec=pltpu.PrefetchScalarGridSpec(
            num_scalar_prefetch=1,
            grid=(tokens // tile,),
            in_specs=in_specs,
            out_specs=[pl.BlockSpec((half, tile), lambda i, idx: (0, i))] * 2,
        ),
        out_shape=[jax.ShapeDtypeStruct((half, tokens), F32)] * 2,
        compiler_params=params(16 * MIB),
        cost_estimate=cost(),
        name="scores",
    )(idx, *args)


def send_y(parts):
    return [lax.ppermute(parts[j], "tensor", y_shift(j)) for j in (1, 3, 2)]


def sum_y(part, got):
    return (part + got[2]) + (got[0] + got[1])


def body(activations, down_weight, output_grads, act_factors, grad_factors, rank_weight):
    tokens = activations.shape[0]
    queries, ranks, hidden = act_factors.shape
    pipe, tensor = lax.axis_index("pipe"), lax.axis_index("tensor")
    x, core, y, z = pipe // 2, pipe % 2, tensor // 2, tensor % 2
    idx = jnp.stack([x, core, y, z]).astype(jnp.int32)
    gf = grad_factors.reshape(-1, grad_factors.shape[2])

    swap = functools.partial(lax.ppermute, axis_name="pipe", perm=core_swap())
    ring = functools.partial(lax.ppermute, axis_name="pipe", perm=x_ring())
    packed, got, activations, act_factors, rank_weight = pack(
        idx,
        output_grads,
        gf,
        (activations, act_factors.reshape(queries * ranks, hidden), rank_weight),
    )
    got = swap(got)

    near0 = ring(packed)

    at = after(idx, packed)
    pieces = list(act_pieces(at, rank_weight, act_factors, activations))
    got, pieces[0] = lax.optimization_barrier((got, pieces[0]))
    near1 = ring(got)
    own = sum_y(pieces[0], send_y(pieces))

    at = after(idx, pieces[0])
    keep0, send0 = layer(at, activations, down_weight, 0, (192,))
    send0, near0 = lax.optimization_barrier((send0, near0))
    got0 = lax.ppermute(send0, "tensor", z_swap())
    at = after(idx, keep0)
    keep1, send1, keep2, send2 = layer(at, activations, down_weight, 192, (320, 512))

    own, near0, near1, send1 = lax.optimization_barrier((own, near0, near1, send1))
    far = ring(near0[gf.shape[0] // 4 :])
    own = own + lax.ppermute(own, "tensor", z_swap())

    own, send1, got0 = lax.optimization_barrier((own, send1, got0))
    got1 = lax.ppermute(send1, "tensor", z_swap())
    mine = jnp.stack(
        [own] + [lax.ppermute(own, "tensor", y_shift(-j)) for j in (1, 2, 3)]
    )
    mine, far, got1, send2 = lax.optimization_barrier((mine, far, got1, send2))
    other = swap(mine)
    got2 = lax.ppermute(send2, "tensor", z_swap())
    keep1 = jnp.concatenate([keep0 + got0, keep1 + got1], axis=1)
    got1 = send_y(keep1)

    raw, send = scores(idx, output_grads, gf, (near0, near1), far, mine, other, ranks)
    raw = raw + swap(send)
    raw = raw + lax.ppermute(raw, "tensor", y_shift(2))
    raw, got1 = lax.optimization_barrier((raw, got1))
    raw = raw + lax.ppermute(raw, "tensor", y_pair())
    raw = raw + lax.ppermute(raw, "tensor", z_swap())

    square = jnp.sum((raw * raw).reshape(queries, -1, 128), axis=1)
    square, got2 = lax.optimization_barrier((square, got2))
    keep2 = keep2 + got2
    got2 = send_y(keep2)
    square = square + lax.ppermute(square, "dp", dp_shift(2))
    square = square + lax.ppermute(square, "dp", [(i, i ^ 1) for i in range(4)])
    spread = jnp.sum(square, axis=1, keepdims=True) / (tokens * lax.axis_size("dp"))
    influence = raw / jnp.sqrt(spread + 1e-06)
    outputs = [
        sum_y(keep[0], got).astype(jnp.bfloat16)
        for keep, got in ((keep1, got1), (keep2, got2))
    ]
    return (jnp.concatenate(outputs, axis=0), influence.T)


def solution(mesh):
    return jax.shard_map(
        body,
        mesh=mesh,
        in_specs=(
            P("dp", "tensor"),
            P("tensor", "pipe"),
            P("dp", ("pipe", "tensor")),
            P("pipe", None, "tensor"),
            P(None, None, ("pipe", "tensor")),
            P("pipe", None),
        ),
        out_specs=(P("dp", ("pipe", "tensor")), P("dp", "pipe")),
        check_vma=False,
    )
```

```python
import functools
import math

import jax
import jax.numpy as jnp
from jax import lax
from jax.experimental import pallas as pl
from jax.experimental.pallas import tpu as pltpu
from jax.sharding import PartitionSpec as P

F32 = jnp.float32
MIB = 1 << 20
WHOLE = pl.BlockSpec(memory_space=pltpu.VMEM)
PACK_COST = 40 * MIB
ACT_COST = 20 * MIB


def x_ring():
    return [(p, ((p // 2 + 1 - 2 * (p % 2)) % 4) * 2 + p % 2) for p in range(8)]


def core_swap():
    return [(p, p ^ 1) for p in range(8)]


def y_shift(d):
    return [(t, ((t // 2 + d) % 4) * 2 + t % 2) for t in range(8)]


def y_pair():
    return [(t, t ^ 2) for t in range(8)]


def z_swap():
    return [(t, t ^ 1) for t in range(8)]


def dp_shift(d):
    return [(i, (i + d) % 4) for i in range(4)]


def params(limit):
    return pltpu.CompilerParams(vmem_limit_bytes=limit)


def cost(nbytes=0):
    return pl.CostEstimate(flops=0, bytes_accessed=nbytes, transcendentals=0)


def in_hbm(value):
    return pltpu.with_memory_space_constraint(value, pltpu.HBM)


def in_vmem(value):
    return pltpu.with_memory_space_constraint(value, pltpu.VMEM)


def after(value, *others):
    return lax.optimization_barrier((value, *others))[0]


def pack_kernel(idx, og_hbm, gf_hbm, *refs):
    *hbm, mine, other, a, af, weight, og, gf, sems = refs
    held = (a, af, weight)
    copies = [
        pltpu.make_async_copy(src, dst, sems.at[i])
        for i, (src, dst) in enumerate(((og_hbm, og), (gf_hbm, gf), *zip(hbm, held)))
    ]
    for copy in copies:
        copy.start()
    tokens = og.shape[0]
    rows = gf.shape[0] // 4

    def gf_rows(distance):
        start = lax.rem(idx[0] + distance, 4) * rows
        return gf[pl.ds(pl.multiple_of(start, rows), rows), :].astype(F32)

    copies[0].wait()
    wide = og[...].astype(F32)
    other[rows : rows + tokens, :] = wide
    mine[rows : rows + tokens, :] = wide
    copies[1].wait()
    other[:rows, :] = gf_rows(3 - 2 * idx[1])
    mine[:rows, :] = gf_rows(1 + 2 * idx[1])
    mine[rows + tokens :, :] = gf_rows(2)
    for copy in copies[2:]:
        copy.wait()


def pack(idx, og, gf, held):
    tokens, width = og.shape
    rows = gf.shape[0] // 4
    return pl.pallas_call(
        pack_kernel,
        grid_spec=pltpu.PrefetchScalarGridSpec(
            num_scalar_prefetch=1,
            grid=(),
            in_specs=[pl.BlockSpec(memory_space=pltpu.HBM)] * (2 + len(held)),
            out_specs=[WHOLE] * (2 + len(held)),
            scratch_shapes=[
                pltpu.VMEM(og.shape, og.dtype),
                pltpu.VMEM(gf.shape, gf.dtype),
                pltpu.SemaphoreType.DMA((2 + len(held),)),
            ],
        ),
        out_shape=[
            jax.ShapeDtypeStruct((r, width), F32) for r in (tokens + 2 * rows, tokens + rows)
        ]
        + [jax.ShapeDtypeStruct(v.shape, v.dtype) for v in held],
        compiler_params=params(4 * MIB),
        cost_estimate=cost(PACK_COST),
        name="pack",
    )(idx, *map(in_hbm, (og, gf, *held)))


def act_kernel(idx, weight, af, a, out0, out1, out2, out3, scratch, *, scale):
    rows = out0.shape[0]
    tile = scratch.shape[1]
    queries, ranks = weight.shape
    diagonal = lax.broadcasted_iota(jnp.int32, (ranks, ranks), 0) == lax.broadcasted_iota(
        jnp.int32, (ranks, ranks), 1
    )
    column = jnp.concatenate(
        [
            jnp.sum(
                jnp.where(diagonal, weight[q : q + 1, :] * scale, 0.0), axis=1, keepdims=True
            )
            for q in range(queries)
        ],
        axis=0,
    )

    @pl.loop(0, a.shape[0] // tile)
    def _(i):
        at = pl.ds(pl.multiple_of(i * tile, tile), tile)
        scratch[...] = column * lax.dot_general(
            af[...], a[at, :], (((1,), (1,)), ((), ())), preferred_element_type=F32
        )
        for j, out in enumerate((out0, out1, out2, out3)):
            start = pl.multiple_of(lax.rem(idx[2] + j, 4) * rows, rows)
            out[:, at] = scratch[pl.ds(start, rows), :]


def act_pieces(idx, weight, af, a):
    qr, tokens = af.shape[0], a.shape[0]
    return pl.pallas_call(
        functools.partial(act_kernel, scale=1.0 / math.sqrt(weight.shape[1])),
        grid_spec=pltpu.PrefetchScalarGridSpec(
            num_scalar_prefetch=1,
            grid=(),
            in_specs=[WHOLE] * 3,
            out_specs=[WHOLE] * 4,
            scratch_shapes=[pltpu.VMEM((qr, 256), F32)],
        ),
        out_shape=[jax.ShapeDtypeStruct((qr // 4, tokens), F32)] * 4,
        compiler_params=params(8 * MIB),
        cost_estimate=cost(ACT_COST),
        name="act",
    )(idx, weight, in_vmem(af), in_vmem(a))


def layer_kernel(idx, a, w, *outs, blocks):
    width = w.shape[1] // 4

    @pl.loop(0, 4)
    def _(j):
        owner = lax.rem(idx[2] + j, 4)
        acc = jnp.dot(
            a[...],
            w[:, pl.ds(pl.multiple_of(owner * width, width), width)],
            preferred_element_type=F32,
        )
        low, high = acc[:, : width // 2], acc[:, width // 2 :]
        at_low = idx[3] == 0
        at = 0
        for rows, keep, send in zip(blocks, outs[0::2], outs[1::2]):
            keep[j] = jnp.where(at_low, low[at : at + rows], high[at : at + rows])
            send[j] = jnp.where(at_low, high[at : at + rows], low[at : at + rows])
            at += rows
        outs[-1][j] = acc[at:]


def layer(idx, a, w, blocks):
    width = w.shape[1] // 4
    shapes = [(4, rows, width // 2) for rows in blocks for _ in range(2)]
    shapes.append((4, a.shape[0] - sum(blocks), width))
    return pl.pallas_call(
        functools.partial(layer_kernel, blocks=blocks),
        grid_spec=pltpu.PrefetchScalarGridSpec(
            num_scalar_prefetch=1,
            grid=(),
            in_specs=[WHOLE] * 2,
            out_specs=[WHOLE] * len(shapes),
        ),
        out_shape=[jax.ShapeDtypeStruct(shape, F32) for shape in shapes],
        compiler_params=params(8 * MIB),
        cost_estimate=cost(),
        name="layer",
    )(idx, in_vmem(a), in_vmem(w))


def halves_kernel(idx, a, b, c, d, keep, send):
    total = (a[...] + d[...]) + (b[...] + c[...])
    half = keep.shape[1]
    low, high = total[:, :half], total[:, half:]
    keep[...] = jnp.where(idx[3] == 0, low, high)
    send[...] = jnp.where(idx[3] == 0, high, low)


def halves(idx, parts):
    rows, width = parts[0].shape
    return pl.pallas_call(
        halves_kernel,
        grid_spec=pltpu.PrefetchScalarGridSpec(
            num_scalar_prefetch=1, grid=(), in_specs=[WHOLE] * 4, out_specs=[WHOLE] * 2
        ),
        out_shape=[jax.ShapeDtypeStruct((rows, width // 2), F32)] * 2,
        compiler_params=params(8 * MIB),
        cost_estimate=cost(),
        name="halves",
    )(idx, *parts)


def score_kernel(idx, og, gf, a1, b1, a2, b2, a3, b3, mine, other, keep, send, *, ranks):
    bf = jnp.bfloat16
    lhs = jnp.concatenate([gf[...]] + [b[...].astype(bf) for b in (b1, b2, b3)], axis=1)
    rhs = jnp.concatenate([og[...]] + [a[...].astype(bf) for a in (a1, a2, a3)], axis=1)
    grad = lax.dot_general(lhs, rhs, (((1,), (1,)), ((), ())), preferred_element_type=F32)
    rows = mine.shape[1]
    sums = []
    for c in range(2):
        parts = []
        for b in range(4):
            j = lax.rem(b + 4 - idx[2], 4)
            act = jnp.where(idx[1] == c, mine[j], other[j])
            at = (c * 4 + b) * rows
            product = grad[at : at + rows, :] * act
            for q in range(0, rows, ranks):
                parts.append(jnp.sum(product[q : q + ranks], axis=0, keepdims=True))
        sums.append(jnp.concatenate(parts, axis=0))
    keep[...] = jnp.where(idx[1] == 0, sums[0], sums[1])
    send[...] = jnp.where(idx[1] == 0, sums[1], sums[0])


def scores(idx, og, gf, near, far, mine, other, ranks):
    tokens, width = og.shape
    qr = gf.shape[0] // 4
    tile = 512
    assert qr % tile == 0 and tokens % qr == 0
    spec = lambda rows, at: pl.BlockSpec((rows, width), lambda i, idx: (at(i, idx), 0))
    skip = qr // tile
    in_specs = [
        spec(tile, lambda i, idx: i),
        spec(qr, lambda i, idx: idx[0]),
        spec(tile, lambda i, idx: skip + i),
        spec(qr, lambda i, idx: 0),
        spec(tile, lambda i, idx: skip + i),
        spec(qr, lambda i, idx: 0),
        spec(tile, lambda i, idx: i),
        spec(qr, lambda i, idx: tokens // qr),
    ]
    args = [in_hbm(og), in_hbm(gf), near[0], near[0], near[1], near[1], far, far]
    for act in (mine, other):
        in_specs.append(pl.BlockSpec((4, act.shape[1], tile), lambda i, idx: (0, 0, i)))
        args.append(act)
    half = qr // ranks // 2
    return pl.pallas_call(
        functools.partial(score_kernel, ranks=ranks),
        grid_spec=pltpu.PrefetchScalarGridSpec(
            num_scalar_prefetch=1,
            grid=(tokens // tile,),
            in_specs=in_specs,
            out_specs=[pl.BlockSpec((half, tile), lambda i, idx: (0, i))] * 2,
        ),
        out_shape=[jax.ShapeDtypeStruct((half, tokens), F32)] * 2,
        compiler_params=params(16 * MIB),
        cost_estimate=cost(),
        name="scores",
    )(idx, *args)


def send_y(parts):
    return [lax.ppermute(parts[j], "tensor", y_shift(j)) for j in (1, 3, 2)]


def sum_y(part, got):
    return (part + got[2]) + (got[0] + got[1])


def body(activations, down_weight, output_grads, act_factors, grad_factors, rank_weight):
    tokens = activations.shape[0]
    queries, ranks, hidden = act_factors.shape
    pipe, tensor = lax.axis_index("pipe"), lax.axis_index("tensor")
    x, core, y, z = pipe // 2, pipe % 2, tensor // 2, tensor % 2
    idx = jnp.stack([x, core, y, z]).astype(jnp.int32)
    gf = grad_factors.reshape(-1, grad_factors.shape[2])

    swap = functools.partial(lax.ppermute, axis_name="pipe", perm=core_swap())
    ring = functools.partial(lax.ppermute, axis_name="pipe", perm=x_ring())
    packed, got, activations, act_factors, rank_weight = pack(
        idx,
        output_grads,
        gf,
        (activations, act_factors.reshape(queries * ranks, hidden), rank_weight),
    )
    got = swap(got)

    near0 = ring(packed)

    at = after(idx, packed)
    pieces = list(act_pieces(at, rank_weight, act_factors, activations))
    got, pieces[0] = lax.optimization_barrier((got, pieces[0]))
    near1 = ring(got)
    own = sum_y(pieces[0], send_y(pieces))

    at = after(idx, pieces[0])
    keep0, send0, keep1, send1, parts = layer(at, activations, down_weight, (352, 288))

    own, send0 = lax.optimization_barrier((own, send0))
    own = own + lax.ppermute(own, "tensor", z_swap())

    own, send0, near0, near1 = lax.optimization_barrier((own, send0, near0, near1))
    got0 = lax.ppermute(send0, "tensor", z_swap())
    far = ring(near0[gf.shape[0] // 4 :])
    mine = jnp.stack(
        [own] + [lax.ppermute(own, "tensor", y_shift(-j)) for j in (1, 2, 3)]
    )
    mine, far, got0, send1, parts = lax.optimization_barrier((mine, far, got0, send1, parts))
    other = swap(mine)
    got1 = lax.ppermute(send1, "tensor", z_swap())
    got = send_y(parts)

    raw, send = scores(idx, output_grads, gf, (near0, near1), far, mine, other, ranks)
    raw = raw + swap(send)
    raw, got1 = lax.optimization_barrier((raw, got1))
    raw = raw + lax.ppermute(raw, "tensor", z_swap())
    raw = raw + lax.ppermute(raw, "tensor", y_shift(2))
    raw, got = lax.optimization_barrier((raw, got))
    keep, send = halves(idx, [parts[0], *got])
    out1 = (keep + lax.ppermute(send, "tensor", z_swap())).astype(jnp.bfloat16)
    raw = raw + lax.ppermute(raw, "tensor", y_pair())
    raw, keep0, keep1 = lax.optimization_barrier((raw, keep0, keep1))
    keep0 = jnp.concatenate([keep0 + got0, keep1 + got1], axis=1)
    got0 = send_y(keep0)

    square = jnp.sum((raw * raw).reshape(queries, -1, 128), axis=1)
    square = square + lax.ppermute(square, "dp", dp_shift(2))
    square, got0[0], got0[1], got0[2] = lax.optimization_barrier((square, *got0))
    square = square + lax.ppermute(square, "dp", [(i, i ^ 1) for i in range(4)])
    spread = jnp.sum(square, axis=1, keepdims=True) / (tokens * lax.axis_size("dp"))
    influence = raw / jnp.sqrt(spread + 1e-06)
    out0 = sum_y(keep0[0], got0).astype(jnp.bfloat16)
    return (jnp.concatenate([out0, out1], axis=0), influence.T)


def solution(mesh):
    return jax.shard_map(
        body,
        mesh=mesh,
        in_specs=(
            P("dp", "tensor"),
            P("tensor", "pipe"),
            P("dp", ("pipe", "tensor")),
            P("pipe", None, "tensor"),
            P(None, None, ("pipe", "tensor")),
            P("pipe", None),
        ),
        out_specs=(P("dp", ("pipe", "tensor")), P("dp", "pipe")),
        check_vma=False,
    )
```

```python
import functools
import math

import jax
import jax.numpy as jnp
from jax import lax
from jax.experimental import pallas as pl
from jax.experimental.pallas import tpu as pltpu
from jax.sharding import PartitionSpec as P

F32 = jnp.float32
MIB = 1 << 20
WHOLE = pl.BlockSpec(memory_space=pltpu.VMEM)
PACK_COST = 40 * MIB
ACT_COST = 20 * MIB


def x_ring():
    return [(p, ((p // 2 + 1 - 2 * (p % 2)) % 4) * 2 + p % 2) for p in range(8)]


def core_swap():
    return [(p, p ^ 1) for p in range(8)]


def y_shift(d):
    return [(t, ((t // 2 + d) % 4) * 2 + t % 2) for t in range(8)]


def y_pair():
    return [(t, t ^ 2) for t in range(8)]


def z_swap():
    return [(t, t ^ 1) for t in range(8)]


def dp_shift(d):
    return [(i, (i + d) % 4) for i in range(4)]


def params(limit):
    return pltpu.CompilerParams(vmem_limit_bytes=limit)


def cost(nbytes=0):
    return pl.CostEstimate(flops=0, bytes_accessed=nbytes, transcendentals=0)


def in_hbm(value):
    return pltpu.with_memory_space_constraint(value, pltpu.HBM)


def in_vmem(value):
    return pltpu.with_memory_space_constraint(value, pltpu.VMEM)


def after(value, *others):
    return lax.optimization_barrier((value, *others))[0]


def pack_kernel(idx, og_hbm, gf_hbm, *refs):
    *hbm, mine, other, a, af, weight, og, gf, sems = refs
    held = (a, af, weight)
    copies = [
        pltpu.make_async_copy(src, dst, sems.at[i])
        for i, (src, dst) in enumerate(((og_hbm, og), (gf_hbm, gf), *zip(hbm, held)))
    ]
    for copy in copies:
        copy.start()
    tokens = og.shape[0]
    rows = gf.shape[0] // 4

    def gf_rows(distance):
        start = lax.rem(idx[0] + distance, 4) * rows
        return gf[pl.ds(pl.multiple_of(start, rows), rows), :].astype(F32)

    copies[0].wait()
    wide = og[...].astype(F32)
    other[rows : rows + tokens, :] = wide
    mine[rows : rows + tokens, :] = wide
    copies[1].wait()
    other[:rows, :] = gf_rows(3 - 2 * idx[1])
    mine[:rows, :] = gf_rows(1 + 2 * idx[1])
    mine[rows + tokens :, :] = gf_rows(2)
    for copy in copies[2:]:
        copy.wait()


def pack(idx, og, gf, held):
    tokens, width = og.shape
    rows = gf.shape[0] // 4
    return pl.pallas_call(
        pack_kernel,
        grid_spec=pltpu.PrefetchScalarGridSpec(
            num_scalar_prefetch=1,
            grid=(),
            in_specs=[pl.BlockSpec(memory_space=pltpu.HBM)] * (2 + len(held)),
            out_specs=[WHOLE] * (2 + len(held)),
            scratch_shapes=[
                pltpu.VMEM(og.shape, og.dtype),
                pltpu.VMEM(gf.shape, gf.dtype),
                pltpu.SemaphoreType.DMA((2 + len(held),)),
            ],
        ),
        out_shape=[
            jax.ShapeDtypeStruct((r, width), F32) for r in (tokens + 2 * rows, tokens + rows)
        ]
        + [jax.ShapeDtypeStruct(v.shape, v.dtype) for v in held],
        compiler_params=params(4 * MIB),
        cost_estimate=cost(PACK_COST),
        name="pack",
    )(idx, *map(in_hbm, (og, gf, *held)))


def act_kernel(idx, weight, af, a, out0, out1, out2, out3, scratch, *, scale):
    rows = out0.shape[0]
    tile = scratch.shape[1]
    queries, ranks = weight.shape
    diagonal = lax.broadcasted_iota(jnp.int32, (ranks, ranks), 0) == lax.broadcasted_iota(
        jnp.int32, (ranks, ranks), 1
    )
    column = jnp.concatenate(
        [
            jnp.sum(
                jnp.where(diagonal, weight[q : q + 1, :] * scale, 0.0), axis=1, keepdims=True
            )
            for q in range(queries)
        ],
        axis=0,
    )

    @pl.loop(0, a.shape[0] // tile)
    def _(i):
        at = pl.ds(pl.multiple_of(i * tile, tile), tile)
        scratch[...] = column * lax.dot_general(
            af[...], a[at, :], (((1,), (1,)), ((), ())), preferred_element_type=F32
        )
        for j, out in enumerate((out0, out1, out2, out3)):
            start = pl.multiple_of(lax.rem(idx[2] + j, 4) * rows, rows)
            out[:, at] = scratch[pl.ds(start, rows), :]


def act_pieces(idx, weight, af, a):
    qr, tokens = af.shape[0], a.shape[0]
    return pl.pallas_call(
        functools.partial(act_kernel, scale=1.0 / math.sqrt(weight.shape[1])),
        grid_spec=pltpu.PrefetchScalarGridSpec(
            num_scalar_prefetch=1,
            grid=(),
            in_specs=[WHOLE] * 3,
            out_specs=[WHOLE] * 4,
            scratch_shapes=[pltpu.VMEM((qr, 256), F32)],
        ),
        out_shape=[jax.ShapeDtypeStruct((qr // 4, tokens), F32)] * 4,
        compiler_params=params(8 * MIB),
        cost_estimate=cost(ACT_COST),
        name="act",
    )(idx, weight, in_vmem(af), in_vmem(a))


def layer_kernel(idx, a, w, *outs, blocks):
    width = w.shape[1] // 4

    @pl.loop(0, 4)
    def _(j):
        owner = lax.rem(idx[2] + j, 4)
        acc = jnp.dot(
            a[...],
            w[:, pl.ds(pl.multiple_of(owner * width, width), width)],
            preferred_element_type=F32,
        )
        low, high = acc[:, : width // 2], acc[:, width // 2 :]
        at_low = idx[3] == 0
        at = 0
        for rows, keep, send in zip(blocks, outs[0::2], outs[1::2]):
            keep[j] = jnp.where(at_low, low[at : at + rows], high[at : at + rows])
            send[j] = jnp.where(at_low, high[at : at + rows], low[at : at + rows])
            at += rows
        outs[-1][j] = acc[at:]


def layer(idx, a, w, blocks):
    width = w.shape[1] // 4
    shapes = [(4, rows, width // 2) for rows in blocks for _ in range(2)]
    shapes.append((4, a.shape[0] - sum(blocks), width))
    return pl.pallas_call(
        functools.partial(layer_kernel, blocks=blocks),
        grid_spec=pltpu.PrefetchScalarGridSpec(
            num_scalar_prefetch=1,
            grid=(),
            in_specs=[WHOLE] * 2,
            out_specs=[WHOLE] * len(shapes),
        ),
        out_shape=[jax.ShapeDtypeStruct(shape, F32) for shape in shapes],
        compiler_params=params(8 * MIB),
        cost_estimate=cost(),
        name="layer",
    )(idx, in_vmem(a), in_vmem(w))


def halves_kernel(idx, a, b, c, d, keep, send):
    total = (a[...] + d[...]) + (b[...] + c[...])
    half = keep.shape[1]
    low, high = total[:, :half], total[:, half:]
    keep[...] = jnp.where(idx[3] == 0, low, high)
    send[...] = jnp.where(idx[3] == 0, high, low)


def halves(idx, parts):
    rows, width = parts[0].shape
    return pl.pallas_call(
        halves_kernel,
        grid_spec=pltpu.PrefetchScalarGridSpec(
            num_scalar_prefetch=1, grid=(), in_specs=[WHOLE] * 4, out_specs=[WHOLE] * 2
        ),
        out_shape=[jax.ShapeDtypeStruct((rows, width // 2), F32)] * 2,
        compiler_params=params(8 * MIB),
        cost_estimate=cost(),
        name="halves",
    )(idx, *parts)


def score_kernel(idx, og, gf, a1, b1, a2, b2, a3, b3, mine, other, keep, send, *, ranks):
    bf = jnp.bfloat16
    lhs = jnp.concatenate([gf[...]] + [b[...].astype(bf) for b in (b1, b2, b3)], axis=1)
    rhs = jnp.concatenate([og[...]] + [a[...].astype(bf) for a in (a1, a2, a3)], axis=1)
    grad = lax.dot_general(lhs, rhs, (((1,), (1,)), ((), ())), preferred_element_type=F32)
    rows = mine.shape[1]
    sums = []
    for c in range(2):
        parts = []
        for b in range(4):
            j = lax.rem(b + 4 - idx[2], 4)
            act = jnp.where(idx[1] == c, mine[j], other[j])
            at = (c * 4 + b) * rows
            product = grad[at : at + rows, :] * act
            for q in range(0, rows, ranks):
                parts.append(jnp.sum(product[q : q + ranks], axis=0, keepdims=True))
        sums.append(jnp.concatenate(parts, axis=0))
    keep[...] = jnp.where(idx[1] == 0, sums[0], sums[1])
    send[...] = jnp.where(idx[1] == 0, sums[1], sums[0])


def scores(idx, og, gf, near, far, mine, other, ranks):
    tokens, width = og.shape
    qr = gf.shape[0] // 4
    tile = 512
    assert qr % tile == 0 and tokens % qr == 0
    spec = lambda rows, at: pl.BlockSpec((rows, width), lambda i, idx: (at(i, idx), 0))
    skip = qr // tile
    in_specs = [
        spec(tile, lambda i, idx: i),
        spec(qr, lambda i, idx: idx[0]),
        spec(tile, lambda i, idx: skip + i),
        spec(qr, lambda i, idx: 0),
        spec(tile, lambda i, idx: skip + i),
        spec(qr, lambda i, idx: 0),
        spec(tile, lambda i, idx: i),
        spec(qr, lambda i, idx: tokens // qr),
    ]
    args = [in_hbm(og), in_hbm(gf), near[0], near[0], near[1], near[1], far, far]
    for act in (mine, other):
        in_specs.append(pl.BlockSpec((4, act.shape[1], tile), lambda i, idx: (0, 0, i)))
        args.append(act)
    half = qr // ranks // 2
    return pl.pallas_call(
        functools.partial(score_kernel, ranks=ranks),
        grid_spec=pltpu.PrefetchScalarGridSpec(
            num_scalar_prefetch=1,
            grid=(tokens // tile,),
            in_specs=in_specs,
            out_specs=[pl.BlockSpec((half, tile), lambda i, idx: (0, i))] * 2,
        ),
        out_shape=[jax.ShapeDtypeStruct((half, tokens), F32)] * 2,
        compiler_params=params(16 * MIB),
        cost_estimate=cost(),
        name="scores",
    )(idx, *args)


def send_y(parts):
    return [lax.ppermute(parts[j], "tensor", y_shift(j)) for j in (1, 3, 2)]


def sum_y(part, got):
    return (part + got[2]) + (got[0] + got[1])


def body(activations, down_weight, output_grads, act_factors, grad_factors, rank_weight):
    tokens = activations.shape[0]
    queries, ranks, hidden = act_factors.shape
    pipe, tensor = lax.axis_index("pipe"), lax.axis_index("tensor")
    x, core, y, z = pipe // 2, pipe % 2, tensor // 2, tensor % 2
    idx = jnp.stack([x, core, y, z]).astype(jnp.int32)
    gf = grad_factors.reshape(-1, grad_factors.shape[2])

    swap = functools.partial(lax.ppermute, axis_name="pipe", perm=core_swap())
    ring = functools.partial(lax.ppermute, axis_name="pipe", perm=x_ring())
    packed, got, activations, act_factors, rank_weight = pack(
        idx,
        output_grads,
        gf,
        (activations, act_factors.reshape(queries * ranks, hidden), rank_weight),
    )
    got = swap(got)

    near0 = ring(packed)

    at = after(idx, packed)
    pieces = list(act_pieces(at, rank_weight, act_factors, activations))
    got, pieces[0] = lax.optimization_barrier((got, pieces[0]))
    near1 = ring(got)
    own = sum_y(pieces[0], send_y(pieces))

    at = after(idx, pieces[0])
    keep0, send0, keep1, send1, parts = layer(at, activations, down_weight, (352, 304))

    own, send0 = lax.optimization_barrier((own, send0))
    own = own + lax.ppermute(own, "tensor", z_swap())

    own, send0, near0, near1 = lax.optimization_barrier((own, send0, near0, near1))
    got0 = lax.ppermute(send0, "tensor", z_swap())
    far = ring(near0[gf.shape[0] // 4 :])
    mine = jnp.stack(
        [own] + [lax.ppermute(own, "tensor", y_shift(-j)) for j in (1, 2, 3)]
    )
    mine, far, got0, send1, parts = lax.optimization_barrier((mine, far, got0, send1, parts))
    other = swap(mine)
    got1 = lax.ppermute(send1, "tensor", z_swap())
    got = send_y(parts)

    raw, send = scores(idx, output_grads, gf, (near0, near1), far, mine, other, ranks)
    raw = raw + swap(send)
    raw = raw + lax.ppermute(raw, "tensor", z_swap())
    raw = raw + lax.ppermute(raw, "tensor", y_shift(2))
    raw, got, got1 = lax.optimization_barrier((raw, got, got1))
    keep, send = halves(idx, [parts[0], *got])
    out1 = (keep + lax.ppermute(send, "tensor", z_swap())).astype(jnp.bfloat16)
    raw = raw + lax.ppermute(raw, "tensor", y_pair())
    raw, keep0, keep1 = lax.optimization_barrier((raw, keep0, keep1))
    keep0 = jnp.concatenate([keep0 + got0, keep1 + got1], axis=1)
    got0 = send_y(keep0)

    square = jnp.sum((raw * raw).reshape(queries, -1, 128), axis=1)
    square = square + lax.ppermute(square, "dp", dp_shift(2))
    square, got0[0], got0[1], got0[2] = lax.optimization_barrier((square, *got0))
    square = square + lax.ppermute(square, "dp", [(i, i ^ 1) for i in range(4)])
    spread = jnp.sum(square, axis=1, keepdims=True) / (tokens * lax.axis_size("dp"))
    influence = raw / jnp.sqrt(spread + 1e-06)
    out0 = sum_y(keep0[0], got0).astype(jnp.bfloat16)
    return (jnp.concatenate([out0, out1], axis=0), influence.T)


def solution(mesh):
    return jax.shard_map(
        body,
        mesh=mesh,
        in_specs=(
            P("dp", "tensor"),
            P("tensor", "pipe"),
            P("dp", ("pipe", "tensor")),
            P("pipe", None, "tensor"),
            P(None, None, ("pipe", "tensor")),
            P("pipe", None),
        ),
        out_specs=(P("dp", ("pipe", "tensor")), P("dp", "pipe")),
        check_vma=False,
    )
```

```python
import functools
import math

import jax
import jax.numpy as jnp
from jax import lax
from jax.experimental import pallas as pl
from jax.experimental.pallas import tpu as pltpu
from jax.sharding import PartitionSpec as P

F32 = jnp.float32
MIB = 1 << 20
WHOLE = pl.BlockSpec(memory_space=pltpu.VMEM)
PACK_COST = 40 * MIB
ACT_COST = 20 * MIB


def x_ring():
    return [(p, ((p // 2 + 1 - 2 * (p % 2)) % 4) * 2 + p % 2) for p in range(8)]


def core_swap():
    return [(p, p ^ 1) for p in range(8)]


def y_shift(d):
    return [(t, ((t // 2 + d) % 4) * 2 + t % 2) for t in range(8)]


def y_pair():
    return [(t, t ^ 2) for t in range(8)]


def z_swap():
    return [(t, t ^ 1) for t in range(8)]


def dp_shift(d):
    return [(i, (i + d) % 4) for i in range(4)]


def params(limit):
    return pltpu.CompilerParams(vmem_limit_bytes=limit)


def cost(nbytes=0):
    return pl.CostEstimate(flops=0, bytes_accessed=nbytes, transcendentals=0)


def in_hbm(value):
    return pltpu.with_memory_space_constraint(value, pltpu.HBM)


def in_vmem(value):
    return pltpu.with_memory_space_constraint(value, pltpu.VMEM)


def after(value, *others):
    return lax.optimization_barrier((value, *others))[0]


def pack_kernel(idx, og_hbm, gf_hbm, *refs):
    *hbm, mine, other, a, af, weight, og, gf, sems = refs
    held = (a, af, weight)
    copies = [
        pltpu.make_async_copy(src, dst, sems.at[i])
        for i, (src, dst) in enumerate(((og_hbm, og), (gf_hbm, gf), *zip(hbm, held)))
    ]
    for copy in copies:
        copy.start()
    tokens = og.shape[0]
    rows = gf.shape[0] // 4

    def gf_rows(distance):
        start = lax.rem(idx[0] + distance, 4) * rows
        return gf[pl.ds(pl.multiple_of(start, rows), rows), :].astype(F32)

    copies[0].wait()
    wide = og[...].astype(F32)
    other[rows : rows + tokens, :] = wide
    mine[rows : rows + tokens, :] = wide
    copies[1].wait()
    other[:rows, :] = gf_rows(3 - 2 * idx[1])
    mine[:rows, :] = gf_rows(1 + 2 * idx[1])
    mine[rows + tokens :, :] = gf_rows(2)
    for copy in copies[2:]:
        copy.wait()


def pack(idx, og, gf, held):
    tokens, width = og.shape
    rows = gf.shape[0] // 4
    return pl.pallas_call(
        pack_kernel,
        grid_spec=pltpu.PrefetchScalarGridSpec(
            num_scalar_prefetch=1,
            grid=(),
            in_specs=[pl.BlockSpec(memory_space=pltpu.HBM)] * (2 + len(held)),
            out_specs=[WHOLE] * (2 + len(held)),
            scratch_shapes=[
                pltpu.VMEM(og.shape, og.dtype),
                pltpu.VMEM(gf.shape, gf.dtype),
                pltpu.SemaphoreType.DMA((2 + len(held),)),
            ],
        ),
        out_shape=[
            jax.ShapeDtypeStruct((r, width), F32) for r in (tokens + 2 * rows, tokens + rows)
        ]
        + [jax.ShapeDtypeStruct(v.shape, v.dtype) for v in held],
        compiler_params=params(4 * MIB),
        cost_estimate=cost(PACK_COST),
        name="pack",
    )(idx, *map(in_hbm, (og, gf, *held)))


def act_kernel(idx, weight, af, a, out0, out1, out2, out3, scratch, *, scale):
    rows = out0.shape[0]
    tile = scratch.shape[1]
    queries, ranks = weight.shape
    diagonal = lax.broadcasted_iota(jnp.int32, (ranks, ranks), 0) == lax.broadcasted_iota(
        jnp.int32, (ranks, ranks), 1
    )
    column = jnp.concatenate(
        [
            jnp.sum(
                jnp.where(diagonal, weight[q : q + 1, :] * scale, 0.0), axis=1, keepdims=True
            )
            for q in range(queries)
        ],
        axis=0,
    )

    @pl.loop(0, a.shape[0] // tile)
    def _(i):
        at = pl.ds(pl.multiple_of(i * tile, tile), tile)
        scratch[...] = column * lax.dot_general(
            af[...], a[at, :], (((1,), (1,)), ((), ())), preferred_element_type=F32
        )
        for j, out in enumerate((out0, out1, out2, out3)):
            start = pl.multiple_of(lax.rem(idx[2] + j, 4) * rows, rows)
            out[:, at] = scratch[pl.ds(start, rows), :]


def act_pieces(idx, weight, af, a):
    qr, tokens = af.shape[0], a.shape[0]
    return pl.pallas_call(
        functools.partial(act_kernel, scale=1.0 / math.sqrt(weight.shape[1])),
        grid_spec=pltpu.PrefetchScalarGridSpec(
            num_scalar_prefetch=1,
            grid=(),
            in_specs=[WHOLE] * 3,
            out_specs=[WHOLE] * 4,
            scratch_shapes=[pltpu.VMEM((qr, 256), F32)],
        ),
        out_shape=[jax.ShapeDtypeStruct((qr // 4, tokens), F32)] * 4,
        compiler_params=params(8 * MIB),
        cost_estimate=cost(ACT_COST),
        name="act",
    )(idx, weight, in_vmem(af), in_vmem(a))


def layer_kernel(idx, a, w, *outs, blocks):
    width = w.shape[1] // 4

    @pl.loop(0, 4)
    def _(j):
        owner = lax.rem(idx[2] + j, 4)
        acc = jnp.dot(
            a[...],
            w[:, pl.ds(pl.multiple_of(owner * width, width), width)],
            preferred_element_type=F32,
        )
        low, high = acc[:, : width // 2], acc[:, width // 2 :]
        at_low = idx[3] == 0
        at = 0
        for rows, keep, send in zip(blocks, outs[0::2], outs[1::2]):
            keep[j] = jnp.where(at_low, low[at : at + rows], high[at : at + rows])
            send[j] = jnp.where(at_low, high[at : at + rows], low[at : at + rows])
            at += rows
        outs[-1][j] = acc[at:]


def layer(idx, a, w, blocks):
    width = w.shape[1] // 4
    shapes = [(4, rows, width // 2) for rows in blocks for _ in range(2)]
    shapes.append((4, a.shape[0] - sum(blocks), width))
    return pl.pallas_call(
        functools.partial(layer_kernel, blocks=blocks),
        grid_spec=pltpu.PrefetchScalarGridSpec(
            num_scalar_prefetch=1,
            grid=(),
            in_specs=[WHOLE] * 2,
            out_specs=[WHOLE] * len(shapes),
        ),
        out_shape=[jax.ShapeDtypeStruct(shape, F32) for shape in shapes],
        compiler_params=params(8 * MIB),
        cost_estimate=cost(),
        name="layer",
    )(idx, in_vmem(a), in_vmem(w))


def halves_kernel(idx, a, b, c, d, keep, send):
    total = (a[...] + d[...]) + (b[...] + c[...])
    half = keep.shape[1]
    low, high = total[:, :half], total[:, half:]
    keep[...] = jnp.where(idx[3] == 0, low, high)
    send[...] = jnp.where(idx[3] == 0, high, low)


def halves(idx, parts):
    rows, width = parts[0].shape
    return pl.pallas_call(
        halves_kernel,
        grid_spec=pltpu.PrefetchScalarGridSpec(
            num_scalar_prefetch=1, grid=(), in_specs=[WHOLE] * 4, out_specs=[WHOLE] * 2
        ),
        out_shape=[jax.ShapeDtypeStruct((rows, width // 2), F32)] * 2,
        compiler_params=params(8 * MIB),
        cost_estimate=cost(),
        name="halves",
    )(idx, *parts)


def score_kernel(idx, og, gf, a1, b1, a2, b2, a3, b3, mine, other, keep, send, *, ranks):
    bf = jnp.bfloat16
    lhs = jnp.concatenate([gf[...]] + [b[...].astype(bf) for b in (b1, b2, b3)], axis=1)
    rhs = jnp.concatenate([og[...]] + [a[...].astype(bf) for a in (a1, a2, a3)], axis=1)
    grad = lax.dot_general(lhs, rhs, (((1,), (1,)), ((), ())), preferred_element_type=F32)
    rows = mine.shape[1]
    sums = []
    for c in range(2):
        parts = []
        for b in range(4):
            j = lax.rem(b + 4 - idx[2], 4)
            act = jnp.where(idx[1] == c, mine[j], other[j])
            at = (c * 4 + b) * rows
            product = grad[at : at + rows, :] * act
            for q in range(0, rows, ranks):
                parts.append(jnp.sum(product[q : q + ranks], axis=0, keepdims=True))
        sums.append(jnp.concatenate(parts, axis=0))
    keep[...] = jnp.where(idx[1] == 0, sums[0], sums[1])
    send[...] = jnp.where(idx[1] == 0, sums[1], sums[0])


def scores(idx, og, gf, near, far, mine, other, ranks):
    tokens, width = og.shape
    qr = gf.shape[0] // 4
    tile = 512
    assert qr % tile == 0 and tokens % qr == 0
    spec = lambda rows, at: pl.BlockSpec((rows, width), lambda i, idx: (at(i, idx), 0))
    skip = qr // tile
    in_specs = [
        spec(tile, lambda i, idx: i),
        spec(qr, lambda i, idx: idx[0]),
        spec(tile, lambda i, idx: skip + i),
        spec(qr, lambda i, idx: 0),
        spec(tile, lambda i, idx: skip + i),
        spec(qr, lambda i, idx: 0),
        spec(tile, lambda i, idx: i),
        spec(qr, lambda i, idx: tokens // qr),
    ]
    args = [in_hbm(og), in_hbm(gf), near[0], near[0], near[1], near[1], far, far]
    for act in (mine, other):
        in_specs.append(pl.BlockSpec((4, act.shape[1], tile), lambda i, idx: (0, 0, i)))
        args.append(act)
    half = qr // ranks // 2
    return pl.pallas_call(
        functools.partial(score_kernel, ranks=ranks),
        grid_spec=pltpu.PrefetchScalarGridSpec(
            num_scalar_prefetch=1,
            grid=(tokens // tile,),
            in_specs=in_specs,
            out_specs=[pl.BlockSpec((half, tile), lambda i, idx: (0, i))] * 2,
        ),
        out_shape=[jax.ShapeDtypeStruct((half, tokens), F32)] * 2,
        compiler_params=params(16 * MIB),
        cost_estimate=cost(),
        name="scores",
    )(idx, *args)


def send_y(parts):
    return [lax.ppermute(parts[j], "tensor", y_shift(j)) for j in (1, 3, 2)]


def sum_y(part, got):
    return (part + got[2]) + (got[0] + got[1])


def body(activations, down_weight, output_grads, act_factors, grad_factors, rank_weight):
    tokens = activations.shape[0]
    queries, ranks, hidden = act_factors.shape
    pipe, tensor = lax.axis_index("pipe"), lax.axis_index("tensor")
    x, core, y, z = pipe // 2, pipe % 2, tensor // 2, tensor % 2
    idx = jnp.stack([x, core, y, z]).astype(jnp.int32)
    gf = grad_factors.reshape(-1, grad_factors.shape[2])

    swap = functools.partial(lax.ppermute, axis_name="pipe", perm=core_swap())
    ring = functools.partial(lax.ppermute, axis_name="pipe", perm=x_ring())
    packed, got, activations, act_factors, rank_weight = pack(
        idx,
        output_grads,
        gf,
        (activations, act_factors.reshape(queries * ranks, hidden), rank_weight),
    )
    got = swap(got)

    near0 = ring(packed)

    at = after(idx, packed)
    pieces = list(act_pieces(at, rank_weight, act_factors, activations))
    got, pieces[0] = lax.optimization_barrier((got, pieces[0]))
    near1 = ring(got)
    own = sum_y(pieces[0], send_y(pieces))

    at = after(idx, pieces[0])
    keep0, send0, keep1, send1, parts = layer(at, activations, down_weight, (352, 304))

    own, send0 = lax.optimization_barrier((own, send0))
    own = own + lax.ppermute(own, "tensor", z_swap())

    own, send0, near1 = lax.optimization_barrier((own, send0, near1))
    got0 = lax.ppermute(send0, "tensor", z_swap())
    far = ring(near0[gf.shape[0] // 4 :])
    mine = jnp.stack(
        [own] + [lax.ppermute(own, "tensor", y_shift(-j)) for j in (1, 2, 3)]
    )
    mine, far, got0, send1, parts = lax.optimization_barrier((mine, far, got0, send1, parts))
    other = swap(mine)
    got1 = lax.ppermute(send1, "tensor", z_swap())
    got = send_y(parts)

    raw, send = scores(idx, output_grads, gf, (near0, near1), far, mine, other, ranks)
    raw = raw + swap(send)
    raw = raw + lax.ppermute(raw, "tensor", z_swap())
    raw = raw + lax.ppermute(raw, "tensor", y_shift(2))
    raw, got, got1 = lax.optimization_barrier((raw, got, got1))
    keep, send = halves(idx, [parts[0], *got])
    out1 = (keep + lax.ppermute(send, "tensor", z_swap())).astype(jnp.bfloat16)
    raw = raw + lax.ppermute(raw, "tensor", y_pair())
    raw, keep0, keep1 = lax.optimization_barrier((raw, keep0, keep1))
    keep0 = jnp.concatenate([keep0 + got0, keep1 + got1], axis=1)
    got0 = send_y(keep0)

    square = jnp.sum((raw * raw).reshape(queries, -1, 128), axis=1)
    square = square + lax.ppermute(square, "dp", dp_shift(2))
    square, got0[0], got0[1], got0[2] = lax.optimization_barrier((square, *got0))
    square = square + lax.ppermute(square, "dp", [(i, i ^ 1) for i in range(4)])
    spread = jnp.sum(square, axis=1, keepdims=True) / (tokens * lax.axis_size("dp"))
    influence = raw / jnp.sqrt(spread + 1e-06)
    out0 = sum_y(keep0[0], got0).astype(jnp.bfloat16)
    return (jnp.concatenate([out0, out1], axis=0), influence.T)


def solution(mesh):
    return jax.shard_map(
        body,
        mesh=mesh,
        in_specs=(
            P("dp", "tensor"),
            P("tensor", "pipe"),
            P("dp", ("pipe", "tensor")),
            P("pipe", None, "tensor"),
            P(None, None, ("pipe", "tensor")),
            P("pipe", None),
        ),
        out_specs=(P("dp", ("pipe", "tensor")), P("dp", "pipe")),
        check_vma=False,
    )
```
